128 devices in a mesh: inst: 8 (over z, y_lo), slab: 16 (over y_hi, x, core).
Axes of the slice: x: 4, y: 4 (y_hi: 2, y_lo: 2; y = y_hi * 2 + y_lo), z: 4, core: 2. Of those that a mesh axis runs over, the one named last changes fastest.
Arguments:
- state: bfloat16 [16, 625, 8192], P('inst', None, 'slab'), may hold values from -6 to 6
- volume: float32 [8192], P('slab'), may hold values from 0.5 to 2
- step_size: float32 [8192], P('slab'), may hold values from 0.1 to 0.5
- stiffness: bfloat16 [625, 625], replicated, may hold values from -0.25 to 0.25
- face_coupling: bfloat16 [6, 625, 625], replicated, may hold values from -0.25 to 0.25
- precond: bfloat16 [625, 625], replicated, may hold values from -0.25 to 0.25
- mode_shapes: bfloat16 [8, 625, 8192], P(None, None, 'slab'), may hold values from -2 to 2
- amplitudes: float32 [16, 8], P('inst'), may hold values from -6 to 6
- surface_owner: int32 [8192], replicated, may hold values from 0 to 8191, as said below
- face_links: int32 [6, 8192], P(None, 'slab'), may hold values from 0 to 639
Outputs:
- residual: float32 [16, 625, 8192], P('inst', None, 'slab')
- new_state: float32 [16, 625, 8192], P('inst', None, 'slab')
The draws below stay inside these ranges and needn't reach their ends.
Inputs may be any that keep to these rules, and one draw needn't show every extreme that they name: Surface rows r with r // 512 = s are held by slab s; of the rows of each slab, exactly 32 act on elements of each slab (surface_owner // 512).
All inputs are finite; a program needn't handle non-finite values.
Results may differ from the reference program's by a relative error of at most 0.0023.
Values may be sent and summed in bfloat16 or wider, within the bound.
A program may use at most 128 MiB of HBM per device.

```python
import math
import jax
import jax.numpy as jnp
from jax import lax

NB = 625
NMODE = 8
NT = 16
ELEM_DEV = 512
HALO = 64
ELEMS = 8192
SURF_DEV = 512
SURF = 8192
N_SLAB = 16


def draw_surface_owner(key, part):
    perm_key, elem_key = jax.random.split(jax.random.fold_in(key, 11))
    base_rows = jnp.tile((jnp.arange(SURF_DEV, dtype=jnp.int32) % N_SLAB)[None, :], (N_SLAB, 1))
    row_keys = jax.random.split(perm_key, N_SLAB)
    targets = jax.vmap(lambda row_key, row: jax.random.permutation(row_key, row))(row_keys, base_rows)
    within = jax.random.randint(elem_key, (N_SLAB, SURF_DEV), 0, ELEM_DEV, dtype=jnp.int32)
    return (targets * ELEM_DEV + within).reshape(-1).astype(jnp.int32)


def draw_face_links(key, part):
    cross_key, side_key, inner_key, band_key = jax.random.split(jax.random.fold_in(key, 23), 4)
    shape = (6, ELEMS)
    crossing = jax.random.randint(cross_key, shape, 0, 100, dtype=jnp.int32) < 12
    side = jax.random.randint(side_key, shape, 0, 2, dtype=jnp.int32)
    inner = jax.random.randint(inner_key, shape, HALO, HALO + ELEM_DEV, dtype=jnp.int32)
    band = jax.random.randint(band_key, shape, 0, HALO, dtype=jnp.int32)
    outer = jnp.where(side == 0, band, HALO + ELEM_DEV + band)
    links = jnp.where(crossing, outer, inner)
    position = jnp.arange(ELEMS, dtype=jnp.int32) % ELEM_DEV
    first_face = jnp.where(position == 0, 0, links[0])
    second_face = jnp.where(position == ELEM_DEV - 1, ELEM_DEV + 2 * HALO - 1, links[1])
    links = jnp.concatenate([first_face[None, :], second_face[None, :], links[2:]], axis=0)
    return links.astype(jnp.int32)


def shard_levels(own_key, dims, cuts, least, largest):
    def one(dim, shards_of):
        draws = jax.random.uniform(jax.random.fold_in(jax.random.fold_in(own_key, 6), dim), (shards_of,), jnp.float32, least / len(cuts), largest / len(cuts))
        return jnp.repeat(jnp.exp(draws), dims[dim] // shards_of).reshape((-1,) + (1,) * (len(dims) - dim - 1))

    gain = one(*cuts[0])
    for cut in cuts[1:]:
        gain = gain * one(*cut)
    return gain


def noise(stream_key, shape, deviation, limit, cuts=(), kind=jnp.bfloat16):
    values = deviation * jax.random.normal(stream_key, shape, jnp.float32)
    if cuts:
        values = values * shard_levels(stream_key, shape, cuts, -0.22, 0.18)
    return jnp.clip(values, -limit, limit).astype(kind)


def setup_inputs(seed: int = 0) -> dict:
    key_of = jax.random.split(jax.random.key(seed), 11)
    return {
        "state": noise(key_of[0], (NT, NB, ELEMS), 1.0, 6.0, ((0, 8), (2, 16))),
        "volume": jnp.clip(jnp.exp(math.log(2.0) - 1.3862944 * jax.random.uniform(key_of[1], (ELEMS,), jnp.float32) ** shard_levels(key_of[1], (ELEMS,), ((0, 16),), -0.2, 0.2)), 0.5, 2.0),
        "step_size": jnp.clip(jnp.exp(math.log(0.5) - 1.609438 * jax.random.uniform(key_of[2], (ELEMS,), jnp.float32) ** shard_levels(key_of[2], (ELEMS,), ((0, 16),), -0.2, 0.2)), 0.1, 0.5),
        "stiffness": noise(key_of[3], (NB, NB), NB ** -0.5, 0.25),
        "face_coupling": noise(key_of[4], (6, NB, NB), NB ** -0.5, 0.25),
        "precond": noise(key_of[5], (NB, NB), NB ** -0.5, 0.25),
        "mode_shapes": noise(key_of[6], (NMODE, NB, SURF), NMODE ** -0.5, 2.0, ((2, 16),)),
        "amplitudes": noise(key_of[7], (NT, NMODE), 1.0, 6.0, ((0, 8),), jnp.float32),
        "surface_owner": draw_surface_owner(jax.random.fold_in(key_of[10], 71), 0),
        "face_links": draw_face_links(jax.random.fold_in(key_of[10], 71), 0),
    }


omega_scale = 0.4


def spectral_table(length):
    steps_int = jnp.arange(length, dtype=jnp.int32)
    offset = steps_int[:, None] - steps_int[None, :]
    parity = jnp.remainder(offset, 2).astype(jnp.float32)
    signed = 1.0 - 2.0 * parity
    nonzero = offset != 0
    phases = math.pi * jnp.where(nonzero, offset, 1).astype(jnp.float32) / length
    cotangent = jnp.cos(phases) / jnp.sin(phases)
    return jnp.where(nonzero, 0.5 * omega_scale * signed * cotangent, 0.0).astype(jnp.float32)


def reference(state, volume, step_size, stiffness, face_coupling, precond, mode_shapes, amplitudes, surface_owner, face_links):
    derivative = spectral_table(NT)
    spectral = volume * jnp.einsum("nm,mbe->nbe", derivative, state.astype(jnp.float32), precision=lax.Precision.HIGHEST)
    deflection = jnp.einsum("nk,kbr->nbr", amplitudes, mode_shapes.astype(jnp.float32), precision=lax.Precision.HIGHEST).astype(jnp.bfloat16)
    forcing = jnp.zeros((NT, NB, ELEMS), jnp.float32).at[:, :, surface_owner].add(deflection.astype(jnp.float32))
    padded = jnp.pad(state, ((0, 0), (0, 0), (HALO, HALO)))
    slab_start = (jnp.arange(ELEMS, dtype=jnp.int32) // ELEM_DEV) * ELEM_DEV
    positions = (slab_start[None, :] + face_links).astype(jnp.int32)

    def one_instance(inputs):
        padded_one, spectral_one, forcing_one = inputs
        own_state = padded_one[:, HALO:HALO + ELEMS]
        own_term = jnp.dot(stiffness, own_state, preferred_element_type=jnp.float32)
        face_term = jnp.zeros((NB, ELEMS), jnp.float32)
        for face in range(6):
            face_term = face_term + jnp.dot(face_coupling[face], padded_one[:, positions[face]], preferred_element_type=jnp.float32)
        residual = spectral_one + own_term + face_term - forcing_one
        rounded = residual.astype(jnp.bfloat16)
        change = jnp.dot(precond, rounded, preferred_element_type=jnp.float32)
        new_state = own_state.astype(jnp.float32) - step_size * change
        return residual, new_state

    residual, new_state = lax.map(one_instance, (padded, spectral, forcing))
    return residual, new_state
```

```python
import functools

import jax
import jax.numpy as jnp
import numpy as np
from jax import lax
from jax.experimental import pallas as pl
from jax.experimental.pallas import tpu as pltpu
from jax.sharding import PartitionSpec as P

MESH = pl.DeviceIdType.MESH
F32, BF16 = jnp.float32, jnp.bfloat16

NB = 625
NBP = 640
GRP = 80
LAST = NB - 7 * GRP
NE = 512
HALVES = ((0, 48), (48, 32))
FIRST_FACES = 3


def derivative_blocks():
    n = np.arange(16)
    d = n[:, None] - n[None, :]
    safe = np.where(d == 0, 1, d)
    value = np.where(d == 0, 0.0, 0.2 * (-1.0) ** d / np.tan(np.pi * safe / 16))
    value = np.kron(value, np.eye(16)).astype(np.float32)
    high = value.astype(jnp.bfloat16)
    low = (value - high.astype(np.float32)).astype(jnp.bfloat16)
    return np.stack([high, low])


def dot(a, b):
    return jnp.dot(a, b, preferred_element_type=F32)


def dot_nt(a, b):
    return lax.dot_general(a, b, (((1,), (1,)), ((), ())), preferred_element_type=F32)


def gather_kernel(
    state_hbm,
    ms_hbm,
    stiff_hbm,
    face_hbm,
    deriv_hbm,
    volume_ref,
    amp_ref,
    owner_ref,
    links_ref,
    res_ref,
    xraw,
    xflat,
    x,
    st_in,
    ms_own,
    ms_oth,
    snd_own,
    snd_oth,
    ms_in,
    ret_out,
    ret_in,
    amp_out,
    amp_in,
    fcv,
    stv,
    dv,
    sel,
    placing,
    forcing,
    local_sem,
    st_ssem,
    st_rsem,
    rt_ssem,
    rt_rsem,
    ms_ssem,
    ms_rsem,
    am_ssem,
    am_rsem,
    halo_ssem,
    halo_rsem,
):
    inst = lax.axis_index("inst")
    slab = lax.axis_index("slab")
    zz, yl = inst // 2, inst % 2
    yh, mine = slab // 8, slab % 8
    inst_oth = zz * 2 + (1 - yl)

    def local(src, dst, k):
        return pltpu.make_async_copy(src, dst, local_sem.at[k])

    state_cp = local(state_hbm, xraw.at[pl.ds(0, NB)], 0)
    state_cp.start()

    def ms_head(dst, grp, k):
        return local(ms_hbm.at[pl.ds(grp * GRP, LAST)], dst.at[pl.ds(0, LAST)], k)

    def ms_tail(dst, grp, k):
        return local(
            ms_hbm.at[pl.ds(grp * GRP + LAST, GRP - LAST)], dst.at[pl.ds(LAST, GRP - LAST)], k
        )

    for dst, grp, k in ((ms_own, inst, 1), (ms_oth, inst_oth, 3)):
        ms_head(dst, grp, k).start()

        @pl.when(grp < 7)
        def _():
            ms_tail(dst, grp, k + 1).start()

        @pl.when(grp == 7)
        def _():
            dst[LAST:GRP] = jnp.zeros((GRP - LAST, 8, NE), BF16)

    stiff_cp = local(stiff_hbm, stv, 5)
    stiff_cp.start()
    deriv_cp = local(deriv_hbm, dv, 6)
    deriv_cp.start()
    face_cp = local(face_hbm, fcv, 7)
    face_cp.start()

    def peer(d):
        return ((zz + d // 2) % 4) * 2 + (yl + d % 2) % 2

    order = (4, 5, 2, 6, 3, 7, 1)
    barrier = pltpu.get_barrier_semaphore()

    def greet(i, s):
        pl.semaphore_signal(barrier, inc=1, device_id={"inst": i, "slab": s}, device_id_type=MESH)

    for d in order:
        greet(peer(d), slab)
    for d in range(1, 8):
        greet(inst, yh * 8 + (mine + d) % 8)
    for d in range(8):
        greet(inst_oth, (1 - yh) * 8 + (mine + d) % 8)
    greet(inst, 15 - slab)

    lane8 = lax.broadcasted_iota(jnp.int32, (8, 128), 1)
    row8 = lax.broadcasted_iota(jnp.int32, (8, 128), 0)
    tiled = jnp.zeros((8, 128), F32)
    amp = amp_ref[...]
    for j in range(2):
        for k in range(8):
            tiled = jnp.where((row8 == j) & (lane8 % 8 == k), amp[j : j + 1, k : k + 1], tiled)
    amp_out[...] = tiled
    amp_in[inst] = tiled

    state_cp.wait()
    xraw[NB:NBP] = jnp.zeros((NBP - NB, 8, 128), BF16)

    def split(g, carry):
        rows = xraw[pl.ds(g * GRP, GRP)].astype(F32).reshape(GRP * 8, 128)
        xflat[...] = rows
        for i in range(2):
            for c in range(4):
                part = xflat[pl.ds(c * 2 + i, GRP, stride=8), :]
                x[i, pl.ds(pl.multiple_of(g * GRP, 16), GRP), c * 128 : (c + 1) * 128] = part.astype(BF16)
        return carry

    lax.fori_loop(0, 8, split, 0)

    @pl.when(slab == 0)
    def _():
        x[:, :, 512:640] = jnp.zeros((2, NBP, 128), BF16)

    @pl.when(slab == 15)
    def _():
        x[:, :, 640:768] = jnp.zeros((2, NBP, 128), BF16)

    for i in range(2):
        st_in[inst, i] = x[i, pl.ds(pl.multiple_of(inst * GRP, 16), GRP), 0:NE]

    pl.semaphore_wait(barrier, 23)

    def state_copy(h, d):
        start, size = HALVES[h]
        p = peer(d)
        return pltpu.make_async_remote_copy(
            src_ref=x.at[:, pl.ds(pl.multiple_of(p * GRP + start, 16), size), pl.ds(0, NE)],
            dst_ref=st_in.at[inst, :, pl.ds(start, size), :],
            send_sem=st_ssem.at[h, d],
            recv_sem=st_rsem.at[h, d],
            device_id={"inst": p, "slab": slab},
            device_id_type=MESH,
        )

    def amp_copy(d):
        return pltpu.make_async_remote_copy(
            src_ref=amp_out,
            dst_ref=amp_in.at[inst],
            send_sem=am_ssem.at[d],
            recv_sem=am_rsem.at[d],
            device_id={"inst": peer(d), "slab": slab},
            device_id_type=MESH,
        )

    def halo_copy(k):
        src, dst, to = ((384, 512, slab + 1), (0, 640, slab - 1))[k]
        return pltpu.make_async_remote_copy(
            src_ref=x.at[:, :, pl.ds(src, 128)],
            dst_ref=x.at[:, :, pl.ds(dst, 128)],
            send_sem=halo_ssem.at[k],
            recv_sem=halo_rsem.at[k],
            device_id={"inst": inst, "slab": to},
            device_id_type=MESH,
        )

    for d in order:
        amp_copy(d).start()
    for d in order:
        state_copy(0, d).start()

    @pl.when(slab < 15)
    def _():
        halo_copy(0).start()

    @pl.when(slab > 0)
    def _():
        halo_copy(1).start()

    for d in order:
        state_copy(1, d).start()

    own = jnp.concatenate([owner_ref[pl.ds(c, 16, stride=4), :] for c in range(4)], axis=1)
    target = own // NE
    element = own - target * NE
    row16 = lax.broadcasted_iota(jnp.int32, (16, NE), 0)
    my_target = jnp.sum(jnp.where(row16 == slab, target, 0), axis=0, keepdims=True)
    up_r = lax.broadcasted_iota(jnp.int32, (NE, NE), 0)
    up_c = lax.broadcasted_iota(jnp.int32, (NE, NE), 1)
    upper = jnp.where(up_r < up_c, 1.0, 0.0).astype(BF16)
    match = jnp.where(row16 == my_target, 1.0, 0.0)
    before = dot(match.astype(BF16), upper)
    rank = jnp.sum(match * before, axis=0, keepdims=True)
    slot = my_target * 32 + rank.astype(jnp.int32)
    s_iota = lax.broadcasted_iota(jnp.int32, (256, NE), 0)
    pick_own = jnp.where(s_iota + yh * 256 == slot, 1.0, 0.0).astype(BF16)
    pick_oth = jnp.where(s_iota + (1 - yh) * 256 == slot, 1.0, 0.0).astype(BF16)

    for dst, grp, k in ((ms_own, inst, 1), (ms_oth, inst_oth, 3)):
        ms_head(dst, grp, k).wait()

        @pl.when(grp < 7)
        def _():
            ms_tail(dst, grp, k + 1).wait()

    snd_own[...] = dot_nt(pick_own, ms_own[...].astype(F32).reshape(GRP * 8, NE).astype(BF16)).astype(BF16)
    snd_oth[...] = dot_nt(pick_oth, ms_oth[...].astype(F32).reshape(GRP * 8, NE).astype(BF16)).astype(BF16)

    def ms_copy(d, other):
        idx = (mine + d) % 8
        src = snd_oth if other else snd_own
        return pltpu.make_async_remote_copy(
            src_ref=src.at[pl.ds(pl.multiple_of(idx * 32, 32), 32), :],
            dst_ref=ms_in.at[pl.ds(pl.multiple_of(slab * 32, 32), 32), :],
            send_sem=ms_ssem.at[int(other), d],
            recv_sem=ms_rsem.at[int(other), d],
            device_id={
                "inst": inst_oth if other else inst,
                "slab": ((1 - yh) if other else yh) * 8 + idx,
            },
            device_id_type=MESH,
        )

    for d in range(8):
        ms_copy(d, True).start()
    for d in range(1, 8):
        ms_copy(d, False).start()
    ms_self = local(
        snd_own.at[pl.ds(pl.multiple_of(mine * 32, 32), 32), :],
        ms_in.at[pl.ds(pl.multiple_of(slab * 32, 32), 32), :],
        8,
    )
    ms_self.start()

    hits = jnp.where(target == slab, 1.0, 0.0)
    ranks = dot(hits.astype(BF16), upper)
    ranks = jnp.where(hits > 0.5, ranks, -1.0)
    element_f = element.astype(F32)
    c_iota = lax.broadcasted_iota(jnp.int32, (32, NE), 0).astype(F32)
    e_iota = lax.broadcasted_iota(jnp.int32, (32, NE), 1).astype(F32)
    for s in range(16):
        found = jnp.where(ranks[s : s + 1, :] == c_iota, element_f[s : s + 1, :], 0.0)
        column = jnp.sum(found, axis=1, keepdims=True)
        placing[32 * s : 32 * s + 32, :] = jnp.where(column == e_iota, 1.0, 0.0).astype(BF16)

    links = links_ref[...]
    where_to = jnp.where(links < 64, links + 576, jnp.where(links < 576, links - 64, links + 64))

    def face(f):
        span = lax.broadcasted_iota(jnp.int32, (768, NE), 0)
        sel[...] = jnp.where(span == where_to[f : f + 1, :], 1.0, 0.0).astype(BF16)
        for i in range(2):
            picked = dot(x[i], sel[...]).astype(BF16)
            res_ref[i, 0:NB] += dot(fcv[f], picked[0:NB])

    stiff_cp.wait()
    for i in range(2):
        res_ref[i, 0:NB] = dot(stv[...], x[i, 0:NB, 0:NE])

    for d in order:
        amp_copy(d).wait_recv()
    a_all = jnp.concatenate([amp_in[p, 0:2] for p in range(8)], axis=0)
    a_all = jnp.broadcast_to(a_all[:, None, :], (16, 16, 128)).reshape(256, 128)
    k_row = lax.broadcasted_iota(jnp.int32, (256, 128), 0) % 16
    k_col = lax.broadcasted_iota(jnp.int32, (256, 128), 1) // 8
    a_all = jnp.where(k_row == k_col, a_all, 0.0)
    a_high = a_all.astype(BF16)
    a_low = (a_all - a_high.astype(F32)).astype(BF16)
    a_both = jnp.concatenate([a_high, a_low], axis=1)

    ms_self.wait()
    for d in range(8):
        ms_copy(d, True).wait_recv()
    for d in range(1, 8):
        ms_copy(d, False).wait_recv()
    for q in range(5):
        rows = ms_in[:, 128 * q : 128 * q + 128]
        deflection = dot_nt(a_both, jnp.concatenate([rows, rows], axis=1)).astype(BF16)
        forcing[q] = dot(deflection, placing[...])

    face_cp.wait()

    @pl.when(slab > 0)
    def _():
        halo_copy(0).wait_recv()

    @pl.when(slab < 15)
    def _():
        halo_copy(1).wait_recv()

    for f in range(FIRST_FACES):
        face(f)

    deriv_cp.wait()
    volume = jnp.concatenate([volume_ref[c : c + 1, :] for c in range(4)], axis=1)

    def ret_copy(h, d):
        start, size = HALVES[h]
        p = peer(d)
        return pltpu.make_async_remote_copy(
            src_ref=ret_out.at[p, :, pl.ds(start, size), :],
            dst_ref=ret_in.at[inst, :, pl.ds(start, size), :],
            send_sem=rt_ssem.at[h, d],
            recv_sem=rt_rsem.at[h, d],
            device_id={"inst": p, "slab": slab},
            device_id_type=MESH,
        )

    for h in range(2):
        for d in order:
            state_copy(h, d).wait_recv()
        start, size = HALVES[h]
        for q in range(start // 16, (start + size) // 16):
            block = st_in[:, :, 16 * q : 16 * q + 16, :].reshape(256, NE)
            spectral = dot(dv[0], block) + dot(dv[1], block)
            back = (volume * spectral - forcing[q]).astype(BF16)
            ret_out[:, :, 16 * q : 16 * q + 16, :] = back.reshape(8, 2, 16, NE)
        for d in order:
            ret_copy(h, d).start()

    for i in range(2):
        ret_in[inst, i] = ret_out[inst, i]

    for f in range(FIRST_FACES, 6):
        face(f)

    for h in range(2):
        for d in order:
            ret_copy(h, d).wait_recv()
    for i in range(2):
        for g in range(8):
            res_ref[i, g * GRP : (g + 1) * GRP] += ret_in[g, i].astype(F32)

    for d in order:
        amp_copy(d).wait_send()
        for h in range(2):
            state_copy(h, d).wait_send()
            ret_copy(h, d).wait_send()
    for d in range(8):
        ms_copy(d, True).wait_send()
    for d in range(1, 8):
        ms_copy(d, False).wait_send()

    @pl.when(slab < 15)
    def _():
        halo_copy(0).wait_send()

    @pl.when(slab > 0)
    def _():
        halo_copy(1).wait_send()


BLK = 128


def update_kernel(res_ref, state_ref, step_ref, precond_ref, res_out, new_out, rounded):
    j = pl.program_id(0)

    @pl.when(j == 0)
    def _():
        rounded[...] = res_ref[...].astype(BF16)

    base = pl.multiple_of(j * BLK, BLK)
    for i in range(2):
        change = dot(precond_ref[...], rounded[i, 0:NB])
        for c in range(4):
            lanes = slice(c * 128, (c + 1) * 128)
            rows = pl.ds(c * 2 + i, BLK, stride=8)
            res_out[rows, :] = res_ref[i, pl.ds(base, BLK), lanes]
            new_out[rows, :] = step_ref[c : c + 1, :] * change[:, lanes]
    new_out[...] = state_ref[...].astype(F32).reshape(BLK * 8, 128) - new_out[...]


def body(state, volume, step_size, stiffness, face_coupling, precond, mode_shapes, amplitudes, surface_owner, face_links):
    raw = state.reshape(2, NB, 4, 128).transpose(1, 2, 0, 3).reshape(NB, 8, 128)
    shapes = mode_shapes.transpose(1, 0, 2)
    any_spec = pl.BlockSpec(memory_space=pl.ANY)
    vmem = pl.BlockSpec(memory_space=pltpu.VMEM)
    dma = pltpu.SemaphoreType.DMA
    res = pl.pallas_call(
        gather_kernel,
        out_shape=jax.ShapeDtypeStruct((2, NBP, NE), F32),
        in_specs=[any_spec] * 5 + [vmem] * 4,
        out_specs=vmem,
        scratch_shapes=[
            pltpu.VMEM((NBP, 8, 128), BF16),
            pltpu.VMEM((GRP * 8, 128), F32),
            pltpu.VMEM((2, NBP, 768), BF16),
            pltpu.VMEM((8, 2, GRP, NE), BF16),
            pltpu.VMEM((GRP, 8, NE), BF16),
            pltpu.VMEM((GRP, 8, NE), BF16),
            pltpu.VMEM((256, GRP * 8), BF16),
            pltpu.VMEM((256, GRP * 8), BF16),
            pltpu.VMEM((512, GRP * 8), BF16),
            pltpu.VMEM((8, 2, GRP, NE), BF16),
            pltpu.VMEM((8, 2, GRP, NE), BF16),
            pltpu.VMEM((8, 128), F32),
            pltpu.VMEM((8, 8, 128), F32),
            pltpu.VMEM((6, NB, NB), BF16),
            pltpu.VMEM((NB, NB), BF16),
            pltpu.VMEM((2, 256, 256), BF16),
            pltpu.VMEM((768, NE), BF16),
            pltpu.VMEM((512, NE), BF16),
            pltpu.VMEM((5, 256, NE), F32),
            dma((9,)),
            dma((2, 8)),
            dma((2, 8)),
            dma((2, 8)),
            dma((2, 8)),
            dma((2, 8)),
            dma((2, 8)),
            dma((8,)),
            dma((8,)),
            dma((2,)),
            dma((2,)),
        ],
        compiler_params=pltpu.CompilerParams(
            collective_id=0, has_side_effects=True, vmem_limit_bytes=56 << 20
        ),
        cost_estimate=pl.CostEstimate(flops=13_000_000_000, bytes_accessed=16_000_000, transcendentals=0),
    )(
        raw,
        shapes,
        stiffness,
        face_coupling,
        jnp.asarray(derivative_blocks()),
        volume.reshape(4, 128),
        amplitudes,
        surface_owner.reshape(64, 128),
        face_links,
    )
    steps = pl.cdiv(NB, BLK)
    res_raw, new_raw = pl.pallas_call(
        update_kernel,
        grid=(steps,),
        out_shape=[jax.ShapeDtypeStruct((NB * 8, 128), F32)] * 2,
        in_specs=[
            pl.BlockSpec((2, NBP, NE), lambda j: (0, 0, 0)),
            pl.BlockSpec((BLK, 8, 128), lambda j: (j, 0, 0)),
            pl.BlockSpec((4, 128), lambda j: (0, 0)),
            pl.BlockSpec((BLK, NB), lambda j: (j, 0)),
        ],
        out_specs=[pl.BlockSpec((BLK * 8, 128), lambda j: (j, 0))] * 2,
        scratch_shapes=[pltpu.VMEM((2, NBP, NE), BF16)],
        compiler_params=pltpu.CompilerParams(vmem_limit_bytes=40 << 20),
        cost_estimate=pl.CostEstimate(flops=800_000_000, bytes_accessed=10_000_000, transcendentals=0),
    )(res, raw, step_size.reshape(4, 128), precond)

    def whole(a):
        return a.reshape(NB, 4, 2, 128).transpose(2, 0, 1, 3).reshape(2, NB, NE)

    return whole(res_raw), whole(new_raw)


def solution(mesh):
    return jax.shard_map(
        body,
        mesh=mesh,
        in_specs=(
            P("inst", None, "slab"),
            P("slab"),
            P("slab"),
            P(),
            P(),
            P(),
            P(None, None, "slab"),
            P("inst", None),
            P(),
            P(None, "slab"),
        ),
        out_specs=(P("inst", None, "slab"), P("inst", None, "slab")),
        check_vma=False,
    )
```

```python
import functools

import jax
import jax.numpy as jnp
import numpy as np
from jax import lax
from jax.experimental import pallas as pl
from jax.experimental.pallas import tpu as pltpu
from jax.sharding import PartitionSpec as P

MESH = pl.DeviceIdType.MESH
F32, BF16 = jnp.float32, jnp.bfloat16

NB = 625
NBP = 640
GRP = 80
LAST = NB - 7 * GRP
NE = 512
HALVES = ((0, 48), (48, 32))
FIRST_FACES = 1


def derivative_blocks():
    n = np.arange(16)
    d = n[:, None] - n[None, :]
    safe = np.where(d == 0, 1, d)
    value = np.where(d == 0, 0.0, 0.2 * (-1.0) ** d / np.tan(np.pi * safe / 16))
    value = np.kron(value, np.eye(16)).astype(np.float32)
    high = value.astype(jnp.bfloat16)
    low = (value - high.astype(np.float32)).astype(jnp.bfloat16)
    return np.stack([high, low])


def dot(a, b):
    return jnp.dot(a, b, preferred_element_type=F32)


def dot_nt(a, b):
    return lax.dot_general(a, b, (((1,), (1,)), ((), ())), preferred_element_type=F32)


def gather_kernel(
    state_hbm,
    ms_hbm,
    stiff_hbm,
    face_hbm,
    precond_hbm,
    deriv_hbm,
    volume_ref,
    step_ref,
    amp_ref,
    owner_ref,
    links_ref,
    res_ref,
    new_ref,
    acc,
    rounded,
    pcv,
    xraw,
    xflat,
    x,
    st_in,
    ms_own,
    ms_oth,
    snd_own,
    snd_oth,
    ms_in,
    ret_out,
    ret_in,
    amp_out,
    amp_in,
    fcv,
    stv,
    dv,
    sel,
    placing,
    forcing,
    local_sem,
    st_ssem,
    st_rsem,
    rt_ssem,
    rt_rsem,
    ms_ssem,
    ms_rsem,
    am_ssem,
    am_rsem,
    halo_ssem,
    halo_rsem,
):
    inst = lax.axis_index("inst")
    slab = lax.axis_index("slab")
    zz, yl = inst // 2, inst % 2
    yh, mine = slab // 8, slab % 8
    inst_oth = zz * 2 + (1 - yl)

    def local(src, dst, k):
        return pltpu.make_async_copy(src, dst, local_sem.at[k])

    state_cp = local(state_hbm, xraw.at[pl.ds(0, NB)], 0)
    state_cp.start()

    def ms_head(dst, grp, k):
        return local(ms_hbm.at[pl.ds(grp * GRP, LAST)], dst.at[pl.ds(0, LAST)], k)

    def ms_tail(dst, grp, k):
        return local(
            ms_hbm.at[pl.ds(grp * GRP + LAST, GRP - LAST)], dst.at[pl.ds(LAST, GRP - LAST)], k
        )

    for dst, grp, k in ((ms_own, inst, 1), (ms_oth, inst_oth, 3)):
        ms_head(dst, grp, k).start()

        @pl.when(grp < 7)
        def _():
            ms_tail(dst, grp, k + 1).start()

        @pl.when(grp == 7)
        def _():
            dst[LAST:GRP] = jnp.zeros((GRP - LAST, 8, NE), BF16)

    stiff_cp = local(stiff_hbm, stv, 5)
    stiff_cp.start()
    deriv_cp = local(deriv_hbm, dv, 6)
    deriv_cp.start()
    face_cp = local(face_hbm, fcv, 7)
    face_cp.start()
    precond_cp = local(precond_hbm, pcv, 9)
    precond_cp.start()

    def peer(d):
        return ((zz + d // 2) % 4) * 2 + (yl + d % 2) % 2

    order = (4, 5, 2, 6, 3, 7, 1)
    barrier = pltpu.get_barrier_semaphore()

    def greet(i, s):
        pl.semaphore_signal(barrier, inc=1, device_id={"inst": i, "slab": s}, device_id_type=MESH)

    for d in order:
        greet(peer(d), slab)
    for d in range(1, 8):
        greet(inst, yh * 8 + (mine + d) % 8)
    for d in range(8):
        greet(inst_oth, (1 - yh) * 8 + (mine + d) % 8)
    greet(inst, 15 - slab)

    lane8 = lax.broadcasted_iota(jnp.int32, (8, 128), 1)
    row8 = lax.broadcasted_iota(jnp.int32, (8, 128), 0)
    tiled = jnp.zeros((8, 128), F32)
    amp = amp_ref[...]
    for j in range(2):
        for k in range(8):
            tiled = jnp.where((row8 == j) & (lane8 % 8 == k), amp[j : j + 1, k : k + 1], tiled)
    amp_out[...] = tiled
    amp_in[inst] = tiled

    state_cp.wait()
    xraw[NB:NBP] = jnp.zeros((NBP - NB, 8, 128), BF16)

    def split(g, carry):
        rows = xraw[pl.ds(g * GRP, GRP)].astype(F32).reshape(GRP * 8, 128)
        xflat[...] = rows
        for i in range(2):
            for c in range(4):
                part = xflat[pl.ds(c * 2 + i, GRP, stride=8), :]
                x[i, pl.ds(pl.multiple_of(g * GRP, 16), GRP), c * 128 : (c + 1) * 128] = part.astype(BF16)
        return carry

    lax.fori_loop(0, 8, split, 0)

    @pl.when(slab == 0)
    def _():
        x[:, :, 512:640] = jnp.zeros((2, NBP, 128), BF16)

    @pl.when(slab == 15)
    def _():
        x[:, :, 640:768] = jnp.zeros((2, NBP, 128), BF16)

    for i in range(2):
        st_in[inst, i] = x[i, pl.ds(pl.multiple_of(inst * GRP, 16), GRP), 0:NE]


    def state_copy(h, d):
        start, size = HALVES[h]
        p = peer(d)
        return pltpu.make_async_remote_copy(
            src_ref=x.at[:, pl.ds(pl.multiple_of(p * GRP + start, 16), size), pl.ds(0, NE)],
            dst_ref=st_in.at[inst, :, pl.ds(start, size), :],
            send_sem=st_ssem.at[h, d],
            recv_sem=st_rsem.at[h, d],
            device_id={"inst": p, "slab": slab},
            device_id_type=MESH,
        )

    def amp_copy(d):
        return pltpu.make_async_remote_copy(
            src_ref=amp_out,
            dst_ref=amp_in.at[inst],
            send_sem=am_ssem.at[d],
            recv_sem=am_rsem.at[d],
            device_id={"inst": peer(d), "slab": slab},
            device_id_type=MESH,
        )

    def halo_copy(k):
        src, dst, to = ((384, 512, slab + 1), (0, 640, slab - 1))[k]
        return pltpu.make_async_remote_copy(
            src_ref=x.at[:, :, pl.ds(src, 128)],
            dst_ref=x.at[:, :, pl.ds(dst, 128)],
            send_sem=halo_ssem.at[k],
            recv_sem=halo_rsem.at[k],
            device_id={"inst": inst, "slab": to},
            device_id_type=MESH,
        )

    own = jnp.concatenate([owner_ref[pl.ds(c, 16, stride=4), :] for c in range(4)], axis=1)
    target = own // NE
    element = own - target * NE
    row16 = lax.broadcasted_iota(jnp.int32, (16, NE), 0)
    my_target = jnp.sum(jnp.where(row16 == slab, target, 0), axis=0, keepdims=True)
    up_r = lax.broadcasted_iota(jnp.int32, (NE, NE), 0)
    up_c = lax.broadcasted_iota(jnp.int32, (NE, NE), 1)
    upper = jnp.where(up_r < up_c, 1.0, 0.0).astype(BF16)
    match = jnp.where(row16 == my_target, 1.0, 0.0)
    before = dot(match.astype(BF16), upper)
    rank = jnp.sum(match * before, axis=0, keepdims=True)
    slot = my_target * 32 + rank.astype(jnp.int32)
    s_iota = lax.broadcasted_iota(jnp.int32, (256, NE), 0)
    pick_own = jnp.where(s_iota + yh * 256 == slot, 1.0, 0.0).astype(BF16)
    pick_oth = jnp.where(s_iota + (1 - yh) * 256 == slot, 1.0, 0.0).astype(BF16)

    for dst, grp, k in ((ms_own, inst, 1), (ms_oth, inst_oth, 3)):
        ms_head(dst, grp, k).wait()

        @pl.when(grp < 7)
        def _():
            ms_tail(dst, grp, k + 1).wait()

    snd_own[...] = dot_nt(pick_own, ms_own[...].astype(F32).reshape(GRP * 8, NE).astype(BF16)).astype(BF16)
    snd_oth[...] = dot_nt(pick_oth, ms_oth[...].astype(F32).reshape(GRP * 8, NE).astype(BF16)).astype(BF16)

    def ms_copy(d, other):
        idx = (mine + d) % 8
        src = snd_oth if other else snd_own
        return pltpu.make_async_remote_copy(
            src_ref=src.at[pl.ds(pl.multiple_of(idx * 32, 32), 32), :],
            dst_ref=ms_in.at[pl.ds(pl.multiple_of(slab * 32, 32), 32), :],
            send_sem=ms_ssem.at[int(other), d],
            recv_sem=ms_rsem.at[int(other), d],
            device_id={
                "inst": inst_oth if other else inst,
                "slab": ((1 - yh) if other else yh) * 8 + idx,
            },
            device_id_type=MESH,
        )

    pl.semaphore_wait(barrier, 23)
    for d in order:
        amp_copy(d).start()
    for d in order:
        state_copy(0, d).start()

    @pl.when(slab < 15)
    def _():
        halo_copy(0).start()

    @pl.when(slab > 0)
    def _():
        halo_copy(1).start()

    for d in range(8):
        ms_copy(d, True).start()
    for d in range(1, 8):
        ms_copy(d, False).start()
    for d in order:
        state_copy(1, d).start()
    ms_self = local(
        snd_own.at[pl.ds(pl.multiple_of(mine * 32, 32), 32), :],
        ms_in.at[pl.ds(pl.multiple_of(slab * 32, 32), 32), :],
        8,
    )
    ms_self.start()

    hits = jnp.where(target == slab, 1.0, 0.0)
    ranks = dot(hits.astype(BF16), upper)
    ranks = jnp.where(hits > 0.5, ranks, -1.0)
    element_f = element.astype(F32)
    c_iota = lax.broadcasted_iota(jnp.int32, (32, NE), 0).astype(F32)
    e_iota = lax.broadcasted_iota(jnp.int32, (32, NE), 1).astype(F32)
    for s in range(16):
        found = jnp.where(ranks[s : s + 1, :] == c_iota, element_f[s : s + 1, :], 0.0)
        column = jnp.sum(found, axis=1, keepdims=True)
        placing[32 * s : 32 * s + 32, :] = jnp.where(column == e_iota, 1.0, 0.0).astype(BF16)

    links = links_ref[...]
    where_to = jnp.where(links < 64, links + 576, jnp.where(links < 576, links - 64, links + 64))

    def face(f):
        span = lax.broadcasted_iota(jnp.int32, (768, NE), 0)
        sel[...] = jnp.where(span == where_to[f : f + 1, :], 1.0, 0.0).astype(BF16)
        for i in range(2):
            picked = dot(x[i], sel[...]).astype(BF16)
            acc[i, 0:NB] += dot(fcv[f], picked[0:NB])

    stiff_cp.wait()
    for i in range(2):
        acc[i, 0:NB] = dot(stv[...], x[i, 0:NB, 0:NE])

    for d in order:
        amp_copy(d).wait_recv()
    a_all = jnp.concatenate([amp_in[p, 0:2] for p in range(8)], axis=0)
    a_all = jnp.broadcast_to(a_all[:, None, :], (16, 16, 128)).reshape(256, 128)
    k_row = lax.broadcasted_iota(jnp.int32, (256, 128), 0) % 16
    k_col = lax.broadcasted_iota(jnp.int32, (256, 128), 1) // 8
    a_all = jnp.where(k_row == k_col, a_all, 0.0)
    a_high = a_all.astype(BF16)
    a_low = (a_all - a_high.astype(F32)).astype(BF16)
    a_both = jnp.concatenate([a_high, a_low], axis=1)

    ms_self.wait()
    for d in range(8):
        ms_copy(d, True).wait_recv()
    for d in range(1, 8):
        ms_copy(d, False).wait_recv()
    for q in range(5):
        rows = ms_in[:, 128 * q : 128 * q + 128]
        deflection = dot_nt(a_both, jnp.concatenate([rows, rows], axis=1)).astype(BF16)
        forcing[q] = dot(deflection, placing[...])

    face_cp.wait()

    @pl.when(slab > 0)
    def _():
        halo_copy(0).wait_recv()

    @pl.when(slab < 15)
    def _():
        halo_copy(1).wait_recv()

    for f in range(FIRST_FACES):
        face(f)

    deriv_cp.wait()
    volume = jnp.concatenate([volume_ref[c : c + 1, :] for c in range(4)], axis=1)

    def ret_copy(h, d):
        start, size = HALVES[h]
        p = peer(d)
        return pltpu.make_async_remote_copy(
            src_ref=ret_out.at[p, :, pl.ds(start, size), :],
            dst_ref=ret_in.at[inst, :, pl.ds(start, size), :],
            send_sem=rt_ssem.at[h, d],
            recv_sem=rt_rsem.at[h, d],
            device_id={"inst": p, "slab": slab},
            device_id_type=MESH,
        )

    for h in range(2):
        for d in order:
            state_copy(h, d).wait_recv()
        start, size = HALVES[h]
        for q in range(start // 16, (start + size) // 16):
            block = st_in[:, :, 16 * q : 16 * q + 16, :].reshape(256, NE)
            spectral = dot(dv[0], block) + dot(dv[1], block)
            back = (volume * spectral - forcing[q]).astype(BF16)
            ret_out[:, :, 16 * q : 16 * q + 16, :] = back.reshape(8, 2, 16, NE)
        for d in order:
            ret_copy(h, d).start()

    for i in range(2):
        ret_in[inst, i] = ret_out[inst, i]

    for f in range(FIRST_FACES, 6):
        face(f)

    for h in range(2):
        for d in order:
            ret_copy(h, d).wait_recv()
    precond_cp.wait()
    for i in range(2):
        for g in range(8):
            total = acc[i, g * GRP : (g + 1) * GRP] + ret_in[g, i].astype(F32)
            rounded[i, g * GRP : (g + 1) * GRP] = total.astype(BF16)
            count = GRP if g < 7 else LAST
            for c in range(4):
                res_ref[pl.ds(g * GRP * 8 + c * 2 + i, count, stride=8), :] = total[
                    0:count, c * 128 : (c + 1) * 128
                ]
    for i in range(2):
        change = dot(pcv[...], rounded[i, 0:NB])
        for c in range(4):
            lanes = slice(c * 128, (c + 1) * 128)
            new = x[i, 0:NB, lanes].astype(F32) - step_ref[c : c + 1, :] * change[:, lanes]
            new_ref[pl.ds(c * 2 + i, NB, stride=8), :] = new

    for d in order:
        amp_copy(d).wait_send()
        for h in range(2):
            state_copy(h, d).wait_send()
            ret_copy(h, d).wait_send()
    for d in range(8):
        ms_copy(d, True).wait_send()
    for d in range(1, 8):
        ms_copy(d, False).wait_send()

    @pl.when(slab < 15)
    def _():
        halo_copy(0).wait_send()

    @pl.when(slab > 0)
    def _():
        halo_copy(1).wait_send()


def body(state, volume, step_size, stiffness, face_coupling, precond, mode_shapes, amplitudes, surface_owner, face_links):
    raw = state.reshape(2, NB, 4, 128).transpose(1, 2, 0, 3).reshape(NB, 8, 128)
    shapes = mode_shapes.transpose(1, 0, 2)
    any_spec = pl.BlockSpec(memory_space=pl.ANY)
    vmem = pl.BlockSpec(memory_space=pltpu.VMEM)
    dma = pltpu.SemaphoreType.DMA
    res_raw, new_raw = pl.pallas_call(
        gather_kernel,
        out_shape=[pltpu.VMEM((NB * 8, 128), F32)] * 2,
        in_specs=[any_spec] * 6 + [vmem] * 5,
        out_specs=[vmem] * 2,
        scratch_shapes=[
            pltpu.VMEM((2, NBP, NE), F32),
            pltpu.VMEM((2, NBP, NE), BF16),
            pltpu.VMEM((NB, NB), BF16),
            pltpu.VMEM((NBP, 8, 128), BF16),
            pltpu.VMEM((GRP * 8, 128), F32),
            pltpu.VMEM((2, NBP, 768), BF16),
            pltpu.VMEM((8, 2, GRP, NE), BF16),
            pltpu.VMEM((GRP, 8, NE), BF16),
            pltpu.VMEM((GRP, 8, NE), BF16),
            pltpu.VMEM((256, GRP * 8), BF16),
            pltpu.VMEM((256, GRP * 8), BF16),
            pltpu.VMEM((512, GRP * 8), BF16),
            pltpu.VMEM((8, 2, GRP, NE), BF16),
            pltpu.VMEM((8, 2, GRP, NE), BF16),
            pltpu.VMEM((8, 128), F32),
            pltpu.VMEM((8, 8, 128), F32),
            pltpu.VMEM((6, NB, NB), BF16),
            pltpu.VMEM((NB, NB), BF16),
            pltpu.VMEM((2, 256, 256), BF16),
            pltpu.VMEM((768, NE), BF16),
            pltpu.VMEM((512, NE), BF16),
            pltpu.VMEM((5, 256, NE), F32),
            dma((10,)),
            dma((2, 8)),
            dma((2, 8)),
            dma((2, 8)),
            dma((2, 8)),
            dma((2, 8)),
            dma((2, 8)),
            dma((8,)),
            dma((8,)),
            dma((2,)),
            dma((2,)),
        ],
        compiler_params=pltpu.CompilerParams(
            collective_id=0, has_side_effects=True, vmem_limit_bytes=56 << 20
        ),
        cost_estimate=pl.CostEstimate(flops=13_000_000_000, bytes_accessed=16_000_000, transcendentals=0),
    )(
        raw,
        shapes,
        stiffness,
        face_coupling,
        precond,
        jnp.asarray(derivative_blocks()),
        volume.reshape(4, 128),
        step_size.reshape(4, 128),
        amplitudes,
        surface_owner.reshape(64, 128),
        face_links,
    )
    def whole(a):
        return a.reshape(NB, 4, 2, 128).transpose(2, 0, 1, 3).reshape(2, NB, NE)

    return whole(res_raw), whole(new_raw)


def solution(mesh):
    return jax.shard_map(
        body,
        mesh=mesh,
        in_specs=(
            P("inst", None, "slab"),
            P("slab"),
            P("slab"),
            P(),
            P(),
            P(),
            P(None, None, "slab"),
            P("inst", None),
            P(),
            P(None, "slab"),
        ),
        out_specs=(P("inst", None, "slab"), P("inst", None, "slab")),
        check_vma=False,
    )
```

```python
import functools

import jax
import jax.numpy as jnp
import numpy as np
from jax import lax
from jax.experimental import pallas as pl
from jax.experimental.pallas import tpu as pltpu
from jax.sharding import PartitionSpec as P

MESH = pl.DeviceIdType.MESH
F32, BF16 = jnp.float32, jnp.bfloat16

NB = 625
NBP = 640
GRP = 80
LAST = NB - 7 * GRP
NE = 512
PIECES = ((0, 48), (48, 32))
TAIL = ((0, 48), (48, 32))
FIRST_PIECES = 1
PLAN = (0, 4, 8)


def derivative_blocks():
    n = np.arange(16)
    d = n[:, None] - n[None, :]
    safe = np.where(d == 0, 1, d)
    value = np.where(d == 0, 0.0, 0.2 * (-1.0) ** d / np.tan(np.pi * safe / 16))
    value = np.kron(value, np.eye(16)).astype(np.float32)
    high = value.astype(jnp.bfloat16)
    low = (value - high.astype(np.float32)).astype(jnp.bfloat16)
    return np.stack([high, low])


def dot(a, b):
    return jnp.dot(a, b, preferred_element_type=F32)


def dot_nt(a, b):
    return lax.dot_general(a, b, (((1,), (1,)), ((), ())), preferred_element_type=F32)


def gather_kernel(
    state_hbm,
    ms_hbm,
    stiff_hbm,
    face_hbm,
    precond_hbm,
    deriv_hbm,
    volume_hbm,
    step_hbm,
    amp_hbm,
    owner_hbm,
    links_hbm,
    res_ref,
    new_ref,
    volume_ref,
    step_ref,
    amp_ref,
    owner_ref,
    links_ref,
    acc,
    rounded,
    pcv,
    pc_cols,
    change,
    xraw,
    xflat,
    x,
    halo,
    halo_out,
    st_in,
    ms_own,
    ms_oth,
    snd_own,
    snd_oth,
    ms_in,
    ret_out,
    ret_in,
    amp_out,
    amp_in,
    fcv,
    stv,
    dv,
    sel,
    placing,
    forcing,
    local_sem,
    st_ssem,
    st_rsem,
    rt_ssem,
    rt_rsem,
    ms_ssem,
    ms_rsem,
    am_ssem,
    am_rsem,
    halo_ssem,
    halo_rsem,
):
    inst = lax.axis_index("inst")
    slab = lax.axis_index("slab")
    zz, yl = inst // 2, inst % 2
    yh, mine = slab // 8, slab % 8
    inst_oth = zz * 2 + (1 - yl)

    def local(src, dst, k):
        return pltpu.make_async_copy(src, dst, local_sem.at[k])

    state_cp = local(state_hbm, xraw.at[pl.ds(0, NB)], 0)
    state_cp.start()

    def ms_head(dst, grp, k):
        return local(ms_hbm.at[pl.ds(grp * GRP, LAST)], dst.at[pl.ds(0, LAST)], k)

    def ms_tail(dst, grp, k):
        return local(
            ms_hbm.at[pl.ds(grp * GRP + LAST, GRP - LAST)], dst.at[pl.ds(LAST, GRP - LAST)], k
        )

    small = [
        local(src, dst, 10 + k)
        for k, (src, dst) in enumerate(
            (
                (amp_hbm, amp_ref),
                (owner_hbm, owner_ref),
                (links_hbm, links_ref),
                (volume_hbm, volume_ref),
                (step_hbm, step_ref),
            )
        )
    ]

    def peer(d):
        return ((zz + d // 2) % 4) * 2 + (yl + d % 2) % 2

    order = (4, 5, 2, 6, 3, 7, 1)
    barrier = pltpu.get_barrier_semaphore()

    def greet(i, s):
        pl.semaphore_signal(barrier, inc=1, device_id={"inst": i, "slab": s}, device_id_type=MESH)

    for d in order:
        greet(peer(d), slab)
    for d in range(1, 8):
        greet(inst, yh * 8 + (mine + d) % 8)
    for d in range(8):
        greet(inst_oth, (1 - yh) * 8 + (mine + d) % 8)
    greet(inst, 15 - slab)
    for copy in small:
        copy.start()

    def state_copy(h, d):
        start, size = PIECES[h]
        p = peer(d)
        return pltpu.make_async_remote_copy(
            src_ref=x.at[:, pl.ds(pl.multiple_of(p * GRP + start, 16), size)],
            dst_ref=st_in.at[inst, :, pl.ds(start, size), :],
            send_sem=st_ssem.at[h, d],
            recv_sem=st_rsem.at[h, d],
            device_id={"inst": p, "slab": slab},
            device_id_type=MESH,
        )

    def amp_copy(d):
        return pltpu.make_async_remote_copy(
            src_ref=amp_out,
            dst_ref=amp_in.at[inst],
            send_sem=am_ssem.at[d],
            recv_sem=am_rsem.at[d],
            device_id={"inst": peer(d), "slab": slab},
            device_id_type=MESH,
        )

    def halo_copy(k):
        dst, to = ((0, slab + 1), (128, slab - 1))[k]
        return pltpu.make_async_remote_copy(
            src_ref=halo_out.at[k],
            dst_ref=halo.at[:, pl.ds(dst, 128)],
            send_sem=halo_ssem.at[k],
            recv_sem=halo_rsem.at[k],
            device_id={"inst": inst, "slab": to},
            device_id_type=MESH,
        )

    state_cp.wait()
    for dst, grp, k in ((ms_own, inst, 1), (ms_oth, inst_oth, 3)):
        ms_head(dst, grp, k).start()

        @pl.when(grp < 7)
        def _():
            ms_tail(dst, grp, k + 1).start()

        @pl.when(grp == 7)
        def _():
            dst[LAST:GRP] = jnp.zeros((GRP - LAST, 8, NE), BF16)
    xraw[NB:NBP] = jnp.zeros((NBP - NB, 8, 128), BF16)

    def split(g):
        rows = xraw[pl.ds(g * GRP, GRP)].astype(F32).reshape(GRP * 8, 128)
        xflat[...] = rows
        parts = {}
        for i in range(2):
            for c in range(4):
                part = xflat[pl.ds(c * 2 + i, GRP, stride=8), :]
                x[i, pl.ds(pl.multiple_of(g * GRP, 16), GRP), c * 128 : (c + 1) * 128] = part.astype(BF16)
                parts[c, i] = part
        rows = pl.ds(pl.multiple_of(g * GRP, 16), GRP)
        first = lax.broadcasted_iota(jnp.int32, (GRP, 128), 1) < 64
        high = jnp.where(first, pltpu.roll(parts[3, 0], 64, 1), parts[3, 1])
        low = jnp.where(first, parts[0, 0], pltpu.roll(parts[0, 1], 64, 1))
        halo_out[0, rows, :] = high.astype(BF16)
        halo_out[1, rows, :] = low.astype(BF16)

    pl.semaphore_wait(barrier, 23)
    for d in order:
        split(peer(d))
        for h in range(FIRST_PIECES):
            state_copy(h, d).start()
    split(inst)
    stiff_cp = local(stiff_hbm, stv, 5)
    stiff_cp.start()
    deriv_cp = local(deriv_hbm, dv, 6)
    deriv_cp.start()
    face_cp = local(face_hbm, fcv, 7)
    face_cp.start()
    precond_cp = local(precond_hbm, pcv, 9)
    precond_cp.start()
    @pl.when(slab == 0)
    def _():
        halo[:, 0:128] = jnp.zeros((NBP, 128), BF16)

    @pl.when(slab == 15)
    def _():
        halo[:, 128:256] = jnp.zeros((NBP, 128), BF16)

    for i in range(2):
        st_in[inst, i] = x[i, pl.ds(pl.multiple_of(inst * GRP, 16), GRP)]


    for copy in small:
        copy.wait()

    lane8 = lax.broadcasted_iota(jnp.int32, (8, 128), 1)
    row8 = lax.broadcasted_iota(jnp.int32, (8, 128), 0)
    tiled = jnp.zeros((8, 128), F32)
    amp = amp_ref[...]
    for j in range(2):
        for k in range(8):
            tiled = jnp.where((row8 == j) & (lane8 % 8 == k), amp[j : j + 1, k : k + 1], tiled)
    amp_out[...] = tiled
    amp_in[inst] = tiled

    for d in order:
        amp_copy(d).start()

    own = jnp.concatenate([owner_ref[pl.ds(c, 16, stride=4), :] for c in range(4)], axis=1)
    target = own // NE
    element = own - target * NE
    row16 = lax.broadcasted_iota(jnp.int32, (16, NE), 0)
    my_target = jnp.sum(jnp.where(row16 == slab, target, 0), axis=0, keepdims=True)
    up_r = lax.broadcasted_iota(jnp.int32, (NE, NE), 0)
    up_c = lax.broadcasted_iota(jnp.int32, (NE, NE), 1)
    upper = jnp.where(up_r < up_c, 1.0, 0.0).astype(BF16)
    match = jnp.where(row16 == my_target, 1.0, 0.0)
    before = dot(match.astype(BF16), upper)
    rank = jnp.sum(match * before, axis=0, keepdims=True)
    slot = my_target * 32 + rank.astype(jnp.int32)
    s_iota = lax.broadcasted_iota(jnp.int32, (256, NE), 0)
    pick_own = jnp.where(s_iota + yh * 256 == slot, 1.0, 0.0).astype(BF16)
    pick_oth = jnp.where(s_iota + (1 - yh) * 256 == slot, 1.0, 0.0).astype(BF16)

    for dst, grp, k in ((ms_own, inst, 1), (ms_oth, inst_oth, 3)):
        ms_head(dst, grp, k).wait()

        @pl.when(grp < 7)
        def _():
            ms_tail(dst, grp, k + 1).wait()

    snd_own[...] = dot_nt(pick_own, ms_own[...].astype(F32).reshape(GRP * 8, NE).astype(BF16)).astype(BF16)
    snd_oth[...] = dot_nt(pick_oth, ms_oth[...].astype(F32).reshape(GRP * 8, NE).astype(BF16)).astype(BF16)

    def ms_copy(d, other):
        idx = (mine + d) % 8
        src = snd_oth if other else snd_own
        return pltpu.make_async_remote_copy(
            src_ref=src.at[pl.ds(pl.multiple_of(idx * 32, 32), 32), :],
            dst_ref=ms_in.at[pl.ds(pl.multiple_of(slab * 32, 32), 32), :],
            send_sem=ms_ssem.at[int(other), d],
            recv_sem=ms_rsem.at[int(other), d],
            device_id={
                "inst": inst_oth if other else inst,
                "slab": ((1 - yh) if other else yh) * 8 + idx,
            },
            device_id_type=MESH,
        )

    @pl.when(slab < 15)
    def _():
        halo_copy(0).start()

    @pl.when(slab > 0)
    def _():
        halo_copy(1).start()

    for d in range(8):
        ms_copy(d, True).start()
    for d in range(1, 8):
        ms_copy(d, False).start()
    for h in range(FIRST_PIECES, len(PIECES)):
        for d in order:
            state_copy(h, d).start()
    ms_self = local(
        snd_own.at[pl.ds(pl.multiple_of(mine * 32, 32), 32), :],
        ms_in.at[pl.ds(pl.multiple_of(slab * 32, 32), 32), :],
        8,
    )
    ms_self.start()

    hits = jnp.where(target == slab, 1.0, 0.0)
    ranks = dot(hits.astype(BF16), upper)
    ranks = jnp.where(hits > 0.5, ranks, -1.0)
    element_f = element.astype(F32)
    c_iota = lax.broadcasted_iota(jnp.int32, (32, NE), 0).astype(F32)
    e_iota = lax.broadcasted_iota(jnp.int32, (32, NE), 1).astype(F32)
    for s in range(16):
        found = jnp.where(ranks[s : s + 1, :] == c_iota, element_f[s : s + 1, :], 0.0)
        column = jnp.sum(found, axis=1, keepdims=True)
        placing[32 * s : 32 * s + 32, :] = jnp.where(column == e_iota, 1.0, 0.0).astype(BF16)

    links = links_ref[...]
    inner = jnp.where((links >= 64) & (links < 576), links - 64, -1)
    outer = jnp.where(links < 64, links, jnp.where(links < 576, -256, links - 448))

    def half_face(u):
        f, i = u // 2, u % 2
        span = lax.broadcasted_iota(jnp.int32, (NE, NE), 0)
        if i == 0:
            sel[...] = jnp.where(span == inner[f : f + 1, :], 1.0, 0.0).astype(BF16)
        edge = jnp.where(span[0:256] == outer[f : f + 1, :] + 64 * i, 1.0, 0.0).astype(BF16)
        picked = (dot(x[i], sel[...]) + dot(halo[...], edge)).astype(BF16)
        acc[i, 0:NB] += dot(fcv[f], picked[0:NB])

    acc[:, NB:NBP] = jnp.zeros((2, NBP - NB, NE), F32)
    stiff_cp.wait()
    for i in range(2):
        acc[i, 0:NB] = dot(stv[...], x[i, 0:NB])

    for d in order:
        amp_copy(d).wait_recv()
    a_all = jnp.concatenate([amp_in[p, 0:2] for p in range(8)], axis=0)
    a_all = jnp.broadcast_to(a_all[:, None, :], (16, 16, 128)).reshape(256, 128)
    k_row = lax.broadcasted_iota(jnp.int32, (256, 128), 0) % 16
    k_col = lax.broadcasted_iota(jnp.int32, (256, 128), 1) // 8
    a_all = jnp.where(k_row == k_col, a_all, 0.0)
    a_high = a_all.astype(BF16)
    a_low = (a_all - a_high.astype(F32)).astype(BF16)
    a_both = jnp.concatenate([a_high, a_low], axis=1)

    ms_self.wait()
    for d in range(8):
        ms_copy(d, True).wait_recv()
    for d in range(1, 8):
        ms_copy(d, False).wait_recv()
    for q in range(5):
        rows = ms_in[:, 128 * q : 128 * q + 128]
        deflection = dot_nt(a_both, jnp.concatenate([rows, rows], axis=1)).astype(BF16)
        forcing[q] = dot(deflection, placing[...])

    face_cp.wait()

    @pl.when(slab > 0)
    def _():
        halo_copy(0).wait_recv()

    @pl.when(slab < 15)
    def _():
        halo_copy(1).wait_recv()

    for u in range(PLAN[0]):
        half_face(u)

    deriv_cp.wait()
    volume = jnp.concatenate([volume_ref[c : c + 1, :] for c in range(4)], axis=1)

    def ret_copy(h, d):
        start, size = PIECES[h]
        p = peer(d)
        return pltpu.make_async_remote_copy(
            src_ref=ret_out.at[p, :, pl.ds(start, size), :],
            dst_ref=ret_in.at[inst, :, pl.ds(start, size), :],
            send_sem=rt_ssem.at[h, d],
            recv_sem=rt_rsem.at[h, d],
            device_id={"inst": p, "slab": slab},
            device_id_type=MESH,
        )

    for h in range(len(PIECES)):
        for d in order:
            state_copy(h, d).wait_recv()
        start, size = PIECES[h]
        for q in range(start // 16, (start + size) // 16):
            block = st_in[:, :, 16 * q : 16 * q + 16, :].reshape(256, NE)
            spectral = dot(dv[0], block) + dot(dv[1], block)
            back = (volume * spectral - forcing[q]).astype(BF16)
            ret_out[:, :, 16 * q : 16 * q + 16, :] = back.reshape(8, 2, 16, NE)
        for d in order:
            ret_copy(h, d).start()
        if h == 0:
            for u in range(PLAN[0], PLAN[0] + PLAN[1]):
                half_face(u)

    for i in range(2):
        ret_in[inst, i] = ret_out[inst, i]

    for u in range(PLAN[0] + PLAN[1], 12):
        half_face(u)

    precond_cp.wait()
    p_row = lax.broadcasted_iota(jnp.int32, (NB, NBP), 0)
    p_col = lax.broadcasted_iota(jnp.int32, (NB, NBP), 1)
    p_first = GRP * (p_col // 48) + p_col % 48
    p_second = GRP * ((p_col - 384) // 32) + 48 + (p_col - 384) % 32
    moved = jnp.where(p_row == jnp.where(p_col < 384, p_first, p_second), 1.0, 0.0).astype(BF16)
    pc_cols[...] = dot(pcv[...], moved).astype(BF16)

    for h in range(2):
        start, size = TAIL[h]
        for k, (piece, _) in enumerate(PIECES):
            if start <= piece < start + size:
                for d in order:
                    ret_copy(k, d).wait_recv()
        base = 384 * h
        for i in range(2):
            for g in range(8):
                row = g * GRP + start
                total = acc[i, row : row + size] + ret_in[g, i, start : start + size].astype(F32)
                rounded[i, base + g * size : base + (g + 1) * size] = total.astype(BF16)
                count = min(size, NB - row)
                for c in range(4):
                    res_ref[pl.ds(row * 8 + c * 2 + i, count, stride=8), :] = total[
                        0:count, c * 128 : (c + 1) * 128
                    ]
            part = dot(pc_cols[:, base : base + 8 * size], rounded[i, base : base + 8 * size])
            if h == 0:
                change[i] = part
                continue
            part = part + change[i]
            for c in range(4):
                lanes = slice(c * 128, (c + 1) * 128)
                new = x[i, 0:NB, lanes].astype(F32) - step_ref[c : c + 1, :] * part[:, lanes]
                new_ref[pl.ds(c * 2 + i, NB, stride=8), :] = new

    for d in order:
        amp_copy(d).wait_send()
        for h in range(len(PIECES)):
            state_copy(h, d).wait_send()
            ret_copy(h, d).wait_send()
    for d in range(8):
        ms_copy(d, True).wait_send()
    for d in range(1, 8):
        ms_copy(d, False).wait_send()

    @pl.when(slab < 15)
    def _():
        halo_copy(0).wait_send()

    @pl.when(slab > 0)
    def _():
        halo_copy(1).wait_send()


def write_kernel(res_in, new_in, res_hbm, new_hbm, sem):
    copies = [
        pltpu.make_async_copy(res_in, res_hbm, sem.at[0]),
        pltpu.make_async_copy(new_in, new_hbm, sem.at[1]),
    ]
    for copy in copies:
        copy.start()
    for copy in copies:
        copy.wait()


def body(state, volume, step_size, stiffness, face_coupling, precond, mode_shapes, amplitudes, surface_owner, face_links):
    raw = state.reshape(2, NB, 4, 128).transpose(1, 2, 0, 3).reshape(NB, 8, 128)
    shapes = mode_shapes.transpose(1, 0, 2)
    any_spec = pl.BlockSpec(memory_space=pl.ANY)
    vmem = pl.BlockSpec(memory_space=pltpu.VMEM)
    dma = pltpu.SemaphoreType.DMA
    res_raw, new_raw = pl.pallas_call(
        gather_kernel,
        out_shape=[pltpu.VMEM((NB * 8, 128), F32)] * 2,
        in_specs=[any_spec] * 11,
        out_specs=[vmem] * 2,
        scratch_shapes=[
            pltpu.VMEM((4, 128), F32),
            pltpu.VMEM((4, 128), F32),
            pltpu.VMEM((2, 8), F32),
            pltpu.VMEM((64, 128), jnp.int32),
            pltpu.VMEM((6, NE), jnp.int32),
            pltpu.VMEM((2, NBP, NE), F32),
            pltpu.VMEM((2, NBP, NE), BF16),
            pltpu.VMEM((NB, NB), BF16),
            pltpu.VMEM((NB, NBP), BF16),
            pltpu.VMEM((2, NB, NE), F32),
            pltpu.VMEM((NBP, 8, 128), BF16),
            pltpu.VMEM((GRP * 8, 128), F32),
            pltpu.VMEM((2, NBP, NE), BF16),
            pltpu.VMEM((NBP, 256), BF16),
            pltpu.VMEM((2, NBP, 128), BF16),
            pltpu.VMEM((8, 2, GRP, NE), BF16),
            pltpu.VMEM((GRP, 8, NE), BF16),
            pltpu.VMEM((GRP, 8, NE), BF16),
            pltpu.VMEM((256, GRP * 8), BF16),
            pltpu.VMEM((256, GRP * 8), BF16),
            pltpu.VMEM((512, GRP * 8), BF16),
            pltpu.VMEM((8, 2, GRP, NE), BF16),
            pltpu.VMEM((8, 2, GRP, NE), BF16),
            pltpu.VMEM((8, 128), F32),
            pltpu.VMEM((8, 8, 128), F32),
            pltpu.VMEM((6, NB, NB), BF16),
            pltpu.VMEM((NB, NB), BF16),
            pltpu.VMEM((2, 256, 256), BF16),
            pltpu.VMEM((NE, NE), BF16),
            pltpu.VMEM((512, NE), BF16),
            pltpu.VMEM((5, 256, NE), F32),
            dma((15,)),
            dma((len(PIECES), 8)),
            dma((len(PIECES), 8)),
            dma((len(PIECES), 8)),
            dma((len(PIECES), 8)),
            dma((2, 8)),
            dma((2, 8)),
            dma((8,)),
            dma((8,)),
            dma((2,)),
            dma((2,)),
        ],
        compiler_params=pltpu.CompilerParams(
            collective_id=0, has_side_effects=True, vmem_limit_bytes=56 << 20
        ),
        cost_estimate=pl.CostEstimate(flops=13_000_000_000, bytes_accessed=16_000_000, transcendentals=0),
    )(
        raw,
        shapes,
        stiffness,
        face_coupling,
        precond,
        jnp.asarray(derivative_blocks()),
        volume.reshape(4, 128),
        step_size.reshape(4, 128),
        amplitudes,
        surface_owner.reshape(64, 128),
        face_links,
    )
    res_raw, new_raw = pl.pallas_call(
        write_kernel,
        out_shape=[jax.ShapeDtypeStruct((NB * 8, 128), F32)] * 2,
        in_specs=[vmem] * 2,
        out_specs=[any_spec] * 2,
        scratch_shapes=[dma((2,))],
        compiler_params=pltpu.CompilerParams(vmem_limit_bytes=2 << 20),
        cost_estimate=pl.CostEstimate(flops=0, bytes_accessed=5_000_000, transcendentals=0),
    )(
        pltpu.with_memory_space_constraint(res_raw, pltpu.VMEM),
        pltpu.with_memory_space_constraint(new_raw, pltpu.VMEM),
    )

    def whole(a):
        return a.reshape(NB, 4, 2, 128).transpose(2, 0, 1, 3).reshape(2, NB, NE)

    return whole(res_raw), whole(new_raw)


def solution(mesh):
    return jax.shard_map(
        body,
        mesh=mesh,
        in_specs=(
            P("inst", None, "slab"),
            P("slab"),
            P("slab"),
            P(),
            P(),
            P(),
            P(None, None, "slab"),
            P("inst", None),
            P(),
            P(None, "slab"),
        ),
        out_specs=(P("inst", None, "slab"), P("inst", None, "slab")),
        check_vma=False,
    )
```

```python
import functools

import jax
import jax.numpy as jnp
import numpy as np
from jax import lax
from jax.experimental import pallas as pl
from jax.experimental.pallas import tpu as pltpu
from jax.sharding import PartitionSpec as P

MESH = pl.DeviceIdType.MESH
F32, BF16 = jnp.float32, jnp.bfloat16

NB = 625
NBP = 640
GRP = 80
LAST = NB - 7 * GRP
NE = 512
PIECES = ((0, 48), (48, 32))
TAIL = ((0, 48), (48, 32))
FIRST_PIECES = 1
PLAN = (0, 4, 8)


def derivative_blocks():
    n = np.arange(16)
    d = n[:, None] - n[None, :]
    safe = np.where(d == 0, 1, d)
    value = np.where(d == 0, 0.0, 0.2 * (-1.0) ** d / np.tan(np.pi * safe / 16))
    value = np.kron(value, np.eye(16)).astype(np.float32)
    high = value.astype(jnp.bfloat16)
    low = (value - high.astype(np.float32)).astype(jnp.bfloat16)
    return np.stack([high, low])


def dot(a, b):
    return jnp.dot(a, b, preferred_element_type=F32)


def dot_nt(a, b):
    return lax.dot_general(a, b, (((1,), (1,)), ((), ())), preferred_element_type=F32)


def gather_kernel(
    state_hbm,
    ms_hbm,
    stiff_hbm,
    face_hbm,
    precond_hbm,
    deriv_hbm,
    volume_hbm,
    amp_hbm,
    owner_hbm,
    links_hbm,
    res_ref,
    change,
    rounded,
    pc_cols,
    x,
    volume_ref,
    amp_ref,
    owner_ref,
    links_ref,
    acc,
    pcv,
    xraw,
    xflat,
    halo,
    halo_out,
    st_in,
    ms_own,
    ms_oth,
    snd_own,
    snd_oth,
    ms_in,
    ret_out,
    ret_in,
    amp_out,
    amp_in,
    fcv,
    stv,
    dv,
    sel,
    placing,
    forcing,
    local_sem,
    st_ssem,
    st_rsem,
    rt_ssem,
    rt_rsem,
    ms_ssem,
    ms_rsem,
    am_ssem,
    am_rsem,
    halo_ssem,
    halo_rsem,
):
    inst = lax.axis_index("inst")
    slab = lax.axis_index("slab")
    zz, yl = inst // 2, inst % 2
    yh, mine = slab // 8, slab % 8
    inst_oth = zz * 2 + (1 - yl)

    def local(src, dst, k):
        return pltpu.make_async_copy(src, dst, local_sem.at[k])

    state_cp = local(state_hbm, xraw.at[pl.ds(0, NB)], 0)
    state_cp.start()

    def ms_head(dst, grp, k):
        return local(ms_hbm.at[pl.ds(grp * GRP, LAST)], dst.at[pl.ds(0, LAST)], k)

    def ms_tail(dst, grp, k):
        return local(
            ms_hbm.at[pl.ds(grp * GRP + LAST, GRP - LAST)], dst.at[pl.ds(LAST, GRP - LAST)], k
        )

    small = [
        local(src, dst, 10 + k)
        for k, (src, dst) in enumerate(
            (
                (amp_hbm, amp_ref),
                (owner_hbm, owner_ref),
                (links_hbm, links_ref),
                (volume_hbm, volume_ref),
            )
        )
    ]

    def peer(d):
        return ((zz + d // 2) % 4) * 2 + (yl + d % 2) % 2

    order = (4, 5, 2, 6, 3, 7, 1)
    barrier = pltpu.get_barrier_semaphore()

    def greet(i, s):
        pl.semaphore_signal(barrier, inc=1, device_id={"inst": i, "slab": s}, device_id_type=MESH)

    for d in order:
        greet(peer(d), slab)
    for d in range(1, 8):
        greet(inst, yh * 8 + (mine + d) % 8)
    for d in range(8):
        greet(inst_oth, (1 - yh) * 8 + (mine + d) % 8)
    greet(inst, 15 - slab)
    for copy in small:
        copy.start()

    def state_copy(h, d):
        start, size = PIECES[h]
        p = peer(d)
        return pltpu.make_async_remote_copy(
            src_ref=x.at[:, pl.ds(pl.multiple_of(p * GRP + start, 16), size)],
            dst_ref=st_in.at[inst, :, pl.ds(start, size), :],
            send_sem=st_ssem.at[h, d],
            recv_sem=st_rsem.at[h, d],
            device_id={"inst": p, "slab": slab},
            device_id_type=MESH,
        )

    def amp_copy(d):
        return pltpu.make_async_remote_copy(
            src_ref=amp_out,
            dst_ref=amp_in.at[inst],
            send_sem=am_ssem.at[d],
            recv_sem=am_rsem.at[d],
            device_id={"inst": peer(d), "slab": slab},
            device_id_type=MESH,
        )

    def halo_copy(k):
        dst, to = ((0, slab + 1), (128, slab - 1))[k]
        return pltpu.make_async_remote_copy(
            src_ref=halo_out.at[k],
            dst_ref=halo.at[:, pl.ds(dst, 128)],
            send_sem=halo_ssem.at[k],
            recv_sem=halo_rsem.at[k],
            device_id={"inst": inst, "slab": to},
            device_id_type=MESH,
        )

    state_cp.wait()
    for dst, grp, k in ((ms_own, inst, 1), (ms_oth, inst_oth, 3)):
        ms_head(dst, grp, k).start()

        @pl.when(grp < 7)
        def _():
            ms_tail(dst, grp, k + 1).start()

        @pl.when(grp == 7)
        def _():
            dst[LAST:GRP] = jnp.zeros((GRP - LAST, 8, NE), BF16)
    xraw[NB:NBP] = jnp.zeros((NBP - NB, 8, 128), BF16)

    def split(g):
        rows = xraw[pl.ds(g * GRP, GRP)].astype(F32).reshape(GRP * 8, 128)
        xflat[...] = rows
        parts = {}
        for i in range(2):
            for c in range(4):
                part = xflat[pl.ds(c * 2 + i, GRP, stride=8), :]
                x[i, pl.ds(pl.multiple_of(g * GRP, 16), GRP), c * 128 : (c + 1) * 128] = part.astype(BF16)
                parts[c, i] = part
        rows = pl.ds(pl.multiple_of(g * GRP, 16), GRP)
        first = lax.broadcasted_iota(jnp.int32, (GRP, 128), 1) < 64
        high = jnp.where(first, pltpu.roll(parts[3, 0], 64, 1), parts[3, 1])
        low = jnp.where(first, parts[0, 0], pltpu.roll(parts[0, 1], 64, 1))
        halo_out[0, rows, :] = high.astype(BF16)
        halo_out[1, rows, :] = low.astype(BF16)

    pl.semaphore_wait(barrier, 23)
    for d in order:
        split(peer(d))
        for h in range(FIRST_PIECES):
            state_copy(h, d).start()
    split(inst)
    stiff_cp = local(stiff_hbm, stv, 5)
    stiff_cp.start()
    deriv_cp = local(deriv_hbm, dv, 6)
    deriv_cp.start()
    face_cp = local(face_hbm, fcv, 7)
    face_cp.start()
    precond_cp = local(precond_hbm, pcv, 9)
    precond_cp.start()
    @pl.when(slab == 0)
    def _():
        halo[:, 0:128] = jnp.zeros((NBP, 128), BF16)

    @pl.when(slab == 15)
    def _():
        halo[:, 128:256] = jnp.zeros((NBP, 128), BF16)

    for i in range(2):
        st_in[inst, i] = x[i, pl.ds(pl.multiple_of(inst * GRP, 16), GRP)]


    for copy in small:
        copy.wait()

    lane8 = lax.broadcasted_iota(jnp.int32, (8, 128), 1)
    row8 = lax.broadcasted_iota(jnp.int32, (8, 128), 0)
    tiled = jnp.zeros((8, 128), F32)
    amp = amp_ref[...]
    for j in range(2):
        for k in range(8):
            tiled = jnp.where((row8 == j) & (lane8 % 8 == k), amp[j : j + 1, k : k + 1], tiled)
    amp_out[...] = tiled
    amp_in[inst] = tiled

    for d in order:
        amp_copy(d).start()

    own = jnp.concatenate([owner_ref[pl.ds(c, 16, stride=4), :] for c in range(4)], axis=1)
    target = own // NE
    element = own - target * NE
    row16 = lax.broadcasted_iota(jnp.int32, (16, NE), 0)
    my_target = jnp.sum(jnp.where(row16 == slab, target, 0), axis=0, keepdims=True)
    up_r = lax.broadcasted_iota(jnp.int32, (NE, NE), 0)
    up_c = lax.broadcasted_iota(jnp.int32, (NE, NE), 1)
    upper = jnp.where(up_r < up_c, 1.0, 0.0).astype(BF16)
    match = jnp.where(row16 == my_target, 1.0, 0.0)
    before = dot(match.astype(BF16), upper)
    rank = jnp.sum(match * before, axis=0, keepdims=True)
    slot = my_target * 32 + rank.astype(jnp.int32)
    s_iota = lax.broadcasted_iota(jnp.int32, (256, NE), 0)
    pick_own = jnp.where(s_iota + yh * 256 == slot, 1.0, 0.0).astype(BF16)
    pick_oth = jnp.where(s_iota + (1 - yh) * 256 == slot, 1.0, 0.0).astype(BF16)

    for dst, grp, k in ((ms_own, inst, 1), (ms_oth, inst_oth, 3)):
        ms_head(dst, grp, k).wait()

        @pl.when(grp < 7)
        def _():
            ms_tail(dst, grp, k + 1).wait()

    snd_own[...] = dot_nt(pick_own, ms_own[...].astype(F32).reshape(GRP * 8, NE).astype(BF16)).astype(BF16)
    snd_oth[...] = dot_nt(pick_oth, ms_oth[...].astype(F32).reshape(GRP * 8, NE).astype(BF16)).astype(BF16)

    def ms_copy(d, other):
        idx = (mine + d) % 8
        src = snd_oth if other else snd_own
        return pltpu.make_async_remote_copy(
            src_ref=src.at[pl.ds(pl.multiple_of(idx * 32, 32), 32), :],
            dst_ref=ms_in.at[pl.ds(pl.multiple_of(slab * 32, 32), 32), :],
            send_sem=ms_ssem.at[int(other), d],
            recv_sem=ms_rsem.at[int(other), d],
            device_id={
                "inst": inst_oth if other else inst,
                "slab": ((1 - yh) if other else yh) * 8 + idx,
            },
            device_id_type=MESH,
        )

    @pl.when(slab < 15)
    def _():
        halo_copy(0).start()

    @pl.when(slab > 0)
    def _():
        halo_copy(1).start()

    for d in range(8):
        ms_copy(d, True).start()
    for d in range(1, 8):
        ms_copy(d, False).start()
    for h in range(FIRST_PIECES, len(PIECES)):
        for d in order:
            state_copy(h, d).start()
    ms_self = local(
        snd_own.at[pl.ds(pl.multiple_of(mine * 32, 32), 32), :],
        ms_in.at[pl.ds(pl.multiple_of(slab * 32, 32), 32), :],
        8,
    )
    ms_self.start()

    hits = jnp.where(target == slab, 1.0, 0.0)
    ranks = dot(hits.astype(BF16), upper)
    ranks = jnp.where(hits > 0.5, ranks, -1.0)
    element_f = element.astype(F32)
    c_iota = lax.broadcasted_iota(jnp.int32, (32, NE), 0).astype(F32)
    e_iota = lax.broadcasted_iota(jnp.int32, (32, NE), 1).astype(F32)
    for s in range(16):
        found = jnp.where(ranks[s : s + 1, :] == c_iota, element_f[s : s + 1, :], 0.0)
        column = jnp.sum(found, axis=1, keepdims=True)
        placing[32 * s : 32 * s + 32, :] = jnp.where(column == e_iota, 1.0, 0.0).astype(BF16)

    links = links_ref[...]
    inner = jnp.where((links >= 64) & (links < 576), links - 64, -1)
    outer = jnp.where(links < 64, links, jnp.where(links < 576, -256, links - 448))

    def half_face(u):
        f, i = u // 2, u % 2
        span = lax.broadcasted_iota(jnp.int32, (NE, NE), 0)
        if i == 0:
            sel[...] = jnp.where(span == inner[f : f + 1, :], 1.0, 0.0).astype(BF16)
        edge = jnp.where(span[0:256] == outer[f : f + 1, :] + 64 * i, 1.0, 0.0).astype(BF16)
        picked = (dot(x[i], sel[...]) + dot(halo[...], edge)).astype(BF16)
        acc[i, 0:NB] += dot(fcv[f], picked[0:NB])

    acc[:, NB:NBP] = jnp.zeros((2, NBP - NB, NE), F32)
    stiff_cp.wait()
    for i in range(2):
        acc[i, 0:NB] = dot(stv[...], x[i, 0:NB])

    for d in order:
        amp_copy(d).wait_recv()
    a_all = jnp.concatenate([amp_in[p, 0:2] for p in range(8)], axis=0)
    a_all = jnp.broadcast_to(a_all[:, None, :], (16, 16, 128)).reshape(256, 128)
    k_row = lax.broadcasted_iota(jnp.int32, (256, 128), 0) % 16
    k_col = lax.broadcasted_iota(jnp.int32, (256, 128), 1) // 8
    a_all = jnp.where(k_row == k_col, a_all, 0.0)
    a_high = a_all.astype(BF16)
    a_low = (a_all - a_high.astype(F32)).astype(BF16)
    a_both = jnp.concatenate([a_high, a_low], axis=1)

    ms_self.wait()
    for d in range(8):
        ms_copy(d, True).wait_recv()
    for d in range(1, 8):
        ms_copy(d, False).wait_recv()
    for q in range(5):
        rows = ms_in[:, 128 * q : 128 * q + 128]
        deflection = dot_nt(a_both, jnp.concatenate([rows, rows], axis=1)).astype(BF16)
        forcing[q] = dot(deflection, placing[...])

    face_cp.wait()

    @pl.when(slab > 0)
    def _():
        halo_copy(0).wait_recv()

    @pl.when(slab < 15)
    def _():
        halo_copy(1).wait_recv()

    for u in range(PLAN[0]):
        half_face(u)

    deriv_cp.wait()
    volume = jnp.concatenate([volume_ref[c : c + 1, :] for c in range(4)], axis=1)

    def ret_copy(h, d):
        start, size = PIECES[h]
        p = peer(d)
        return pltpu.make_async_remote_copy(
            src_ref=ret_out.at[p, :, pl.ds(start, size), :],
            dst_ref=ret_in.at[inst, :, pl.ds(start, size), :],
            send_sem=rt_ssem.at[h, d],
            recv_sem=rt_rsem.at[h, d],
            device_id={"inst": p, "slab": slab},
            device_id_type=MESH,
        )

    for h in range(len(PIECES)):
        for d in order:
            state_copy(h, d).wait_recv()
        start, size = PIECES[h]
        for q in range(start // 16, (start + size) // 16):
            block = st_in[:, :, 16 * q : 16 * q + 16, :].reshape(256, NE)
            spectral = dot(dv[0], block) + dot(dv[1], block)
            back = (volume * spectral - forcing[q]).astype(BF16)
            ret_out[:, :, 16 * q : 16 * q + 16, :] = back.reshape(8, 2, 16, NE)
        for d in order:
            ret_copy(h, d).start()
        if h == 0:
            for u in range(PLAN[0], PLAN[0] + PLAN[1]):
                half_face(u)

    for i in range(2):
        ret_in[inst, i] = ret_out[inst, i]

    for u in range(PLAN[0] + PLAN[1], 12):
        half_face(u)

    precond_cp.wait()
    p_row = lax.broadcasted_iota(jnp.int32, (NB, NBP), 0)
    p_col = lax.broadcasted_iota(jnp.int32, (NB, NBP), 1)
    p_first = GRP * (p_col // 48) + p_col % 48
    p_second = GRP * ((p_col - 384) // 32) + 48 + (p_col - 384) % 32
    moved = jnp.where(p_row == jnp.where(p_col < 384, p_first, p_second), 1.0, 0.0).astype(BF16)
    pc_cols[...] = dot(pcv[...], moved).astype(BF16)

    for h in range(2):
        start, size = TAIL[h]
        for k, (piece, _) in enumerate(PIECES):
            if start <= piece < start + size:
                for d in order:
                    ret_copy(k, d).wait_recv()
        base = 384 * h
        for i in range(2):
            for g in range(8):
                row = g * GRP + start
                total = acc[i, row : row + size] + ret_in[g, i, start : start + size].astype(F32)
                rounded[i, base + g * size : base + (g + 1) * size] = total.astype(BF16)
                count = min(size, NB - row)
                for c in range(4):
                    res_ref[pl.ds(row * 8 + c * 2 + i, count, stride=8), :] = total[
                        0:count, c * 128 : (c + 1) * 128
                    ]
            if h == 0:
                change[i] = dot(pc_cols[:, 0:384], rounded[i, 0:384])

    for d in order:
        amp_copy(d).wait_send()
        for h in range(len(PIECES)):
            state_copy(h, d).wait_send()
            ret_copy(h, d).wait_send()
    for d in range(8):
        ms_copy(d, True).wait_send()
    for d in range(1, 8):
        ms_copy(d, False).wait_send()

    @pl.when(slab < 15)
    def _():
        halo_copy(0).wait_send()

    @pl.when(slab > 0)
    def _():
        halo_copy(1).wait_send()


CHUNKS = ((0, 320), (320, 305))


def finish_kernel(res_in, change, rounded, pc_cols, x, step_ref, res_hbm, new_hbm, new, sem):
    copies = [
        pltpu.make_async_copy(res_in.at[pl.ds(8 * b, 8 * n)], res_hbm.at[pl.ds(8 * b, 8 * n)], sem.at[0, k])
        for k, (b, n) in enumerate(CHUNKS)
    ]
    for copy in copies:
        copy.start()
    for k, (b, n) in enumerate(CHUNKS):
        for i in range(2):
            part = dot(pc_cols[b : b + n, 384:640], rounded[i, 384:640]) + change[i, b : b + n]
            for c in range(4):
                lanes = slice(c * 128, (c + 1) * 128)
                value = x[i, b : b + n, lanes].astype(F32) - step_ref[c : c + 1, :] * part[:, lanes]
                new[pl.ds(8 * b + c * 2 + i, n, stride=8), :] = value
        copy = pltpu.make_async_copy(new.at[pl.ds(8 * b, 8 * n)], new_hbm.at[pl.ds(8 * b, 8 * n)], sem.at[1, k])
        copy.start()
        copies.append(copy)
    for copy in copies:
        copy.wait()


def body(state, volume, step_size, stiffness, face_coupling, precond, mode_shapes, amplitudes, surface_owner, face_links):
    raw = state.reshape(2, NB, 4, 128).transpose(1, 2, 0, 3).reshape(NB, 8, 128)
    shapes = mode_shapes.transpose(1, 0, 2)
    any_spec = pl.BlockSpec(memory_space=pl.ANY)
    vmem = pl.BlockSpec(memory_space=pltpu.VMEM)
    dma = pltpu.SemaphoreType.DMA
    held = pl.pallas_call(
        gather_kernel,
        out_shape=[
            pltpu.VMEM((NB * 8, 128), F32),
            pltpu.VMEM((2, NB, NE), F32),
            pltpu.VMEM((2, NBP, NE), BF16),
            pltpu.VMEM((NB, NBP), BF16),
            pltpu.VMEM((2, NBP, NE), BF16),
        ],
        in_specs=[any_spec] * 10,
        out_specs=[vmem] * 5,
        scratch_shapes=[
            pltpu.VMEM((4, 128), F32),
            pltpu.VMEM((2, 8), F32),
            pltpu.VMEM((64, 128), jnp.int32),
            pltpu.VMEM((6, NE), jnp.int32),
            pltpu.VMEM((2, NBP, NE), F32),
            pltpu.VMEM((NB, NB), BF16),
            pltpu.VMEM((NBP, 8, 128), BF16),
            pltpu.VMEM((GRP * 8, 128), F32),
            pltpu.VMEM((NBP, 256), BF16),
            pltpu.VMEM((2, NBP, 128), BF16),
            pltpu.VMEM((8, 2, GRP, NE), BF16),
            pltpu.VMEM((GRP, 8, NE), BF16),
            pltpu.VMEM((GRP, 8, NE), BF16),
            pltpu.VMEM((256, GRP * 8), BF16),
            pltpu.VMEM((256, GRP * 8), BF16),
            pltpu.VMEM((512, GRP * 8), BF16),
            pltpu.VMEM((8, 2, GRP, NE), BF16),
            pltpu.VMEM((8, 2, GRP, NE), BF16),
            pltpu.VMEM((8, 128), F32),
            pltpu.VMEM((8, 8, 128), F32),
            pltpu.VMEM((6, NB, NB), BF16),
            pltpu.VMEM((NB, NB), BF16),
            pltpu.VMEM((2, 256, 256), BF16),
            pltpu.VMEM((NE, NE), BF16),
            pltpu.VMEM((512, NE), BF16),
            pltpu.VMEM((5, 256, NE), F32),
            dma((15,)),
            dma((len(PIECES), 8)),
            dma((len(PIECES), 8)),
            dma((len(PIECES), 8)),
            dma((len(PIECES), 8)),
            dma((2, 8)),
            dma((2, 8)),
            dma((8,)),
            dma((8,)),
            dma((2,)),
            dma((2,)),
        ],
        compiler_params=pltpu.CompilerParams(
            collective_id=0, has_side_effects=True, vmem_limit_bytes=54 << 20
        ),
        cost_estimate=pl.CostEstimate(flops=13_000_000_000, bytes_accessed=16_000_000, transcendentals=0),
    )(
        raw,
        shapes,
        stiffness,
        face_coupling,
        precond,
        jnp.asarray(derivative_blocks()),
        volume.reshape(4, 128),
        amplitudes,
        surface_owner.reshape(64, 128),
        face_links,
    )
    res_raw, new_raw = pl.pallas_call(
        finish_kernel,
        out_shape=[jax.ShapeDtypeStruct((NB * 8, 128), F32)] * 2,
        in_specs=[vmem] * 6,
        out_specs=[any_spec] * 2,
        scratch_shapes=[pltpu.VMEM((NB * 8, 128), F32), dma((2, 2))],
        compiler_params=pltpu.CompilerParams(vmem_limit_bytes=10 << 20),
        cost_estimate=pl.CostEstimate(flops=330_000_000, bytes_accessed=5_000_000, transcendentals=0),
    )(*[pltpu.with_memory_space_constraint(a, pltpu.VMEM) for a in held], step_size.reshape(4, 128))

    def whole(a):
        return a.reshape(NB, 4, 2, 128).transpose(2, 0, 1, 3).reshape(2, NB, NE)

    return whole(res_raw), whole(new_raw)


def solution(mesh):
    return jax.shard_map(
        body,
        mesh=mesh,
        in_specs=(
            P("inst", None, "slab"),
            P("slab"),
            P("slab"),
            P(),
            P(),
            P(),
            P(None, None, "slab"),
            P("inst", None),
            P(),
            P(None, "slab"),
        ),
        out_specs=(P("inst", None, "slab"), P("inst", None, "slab")),
        check_vma=False,
    )
```

```python
import functools

import jax
import jax.numpy as jnp
import numpy as np
from jax import lax
from jax.experimental import pallas as pl
from jax.experimental.pallas import tpu as pltpu
from jax.sharding import PartitionSpec as P

MESH = pl.DeviceIdType.MESH
F32, BF16 = jnp.float32, jnp.bfloat16

NB = 625
NBP = 640
GRP = 80
LAST = NB - 7 * GRP
NE = 512
PIECES = ((0, 48), (48, 32))
TAIL = ((0, 48), (48, 32))
FIRST_PIECES = 1
PLAN = (0, 4, 8)


def derivative_blocks():
    n = np.arange(16)
    d = n[:, None] - n[None, :]
    safe = np.where(d == 0, 1, d)
    value = np.where(d == 0, 0.0, 0.2 * (-1.0) ** d / np.tan(np.pi * safe / 16))
    value = np.kron(value, np.eye(16)).astype(np.float32)
    high = value.astype(jnp.bfloat16)
    low = (value - high.astype(np.float32)).astype(jnp.bfloat16)
    return np.stack([high, low])


def dot(a, b):
    return jnp.dot(a, b, preferred_element_type=F32)


def dot_nt(a, b):
    return lax.dot_general(a, b, (((1,), (1,)), ((), ())), preferred_element_type=F32)


def gather_kernel(
    state_hbm,
    ms_hbm,
    stiff_hbm,
    face_hbm,
    precond_hbm,
    deriv_hbm,
    volume_hbm,
    amp_hbm,
    owner_hbm,
    links_hbm,
    res_ref,
    change,
    rounded,
    pc_cols,
    x,
    volume_ref,
    amp_ref,
    owner_ref,
    links_ref,
    acc,
    pcv,
    xraw,
    xflat,
    halo,
    halo_out,
    st_in,
    ms_own,
    ms_oth,
    snd_own,
    snd_oth,
    ms_in,
    ret_out,
    ret_in,
    amp_out,
    amp_in,
    fcv,
    stv,
    dv,
    sel,
    placing,
    forcing,
    local_sem,
    st_ssem,
    st_rsem,
    rt_ssem,
    rt_rsem,
    ms_ssem,
    ms_rsem,
    am_ssem,
    am_rsem,
    halo_ssem,
    halo_rsem,
):
    inst = lax.axis_index("inst")
    slab = lax.axis_index("slab")
    zz, yl = inst // 2, inst % 2
    yh, mine = slab // 8, slab % 8
    inst_oth = zz * 2 + (1 - yl)

    def local(src, dst, k):
        return pltpu.make_async_copy(src, dst, local_sem.at[k])

    state_cp = local(state_hbm, xraw.at[pl.ds(0, NB)], 0)
    state_cp.start()

    def ms_head(dst, grp, k):
        return local(ms_hbm.at[pl.ds(grp * GRP, LAST)], dst.at[pl.ds(0, LAST)], k)

    def ms_tail(dst, grp, k):
        return local(
            ms_hbm.at[pl.ds(grp * GRP + LAST, GRP - LAST)], dst.at[pl.ds(LAST, GRP - LAST)], k
        )

    small = [
        local(src, dst, 10 + k)
        for k, (src, dst) in enumerate(
            (
                (amp_hbm, amp_ref),
                (owner_hbm, owner_ref),
                (links_hbm, links_ref),
                (volume_hbm, volume_ref),
            )
        )
    ]

    def peer(d):
        return ((zz + d // 2) % 4) * 2 + (yl + d % 2) % 2

    order = (4, 5, 2, 6, 3, 7, 1)
    barrier = pltpu.get_barrier_semaphore()

    def greet(i, s):
        pl.semaphore_signal(barrier, inc=1, device_id={"inst": i, "slab": s}, device_id_type=MESH)

    for d in order:
        greet(peer(d), slab)
    for d in range(1, 8):
        greet(inst, yh * 8 + (mine + d) % 8)
    for d in range(8):
        greet(inst_oth, (1 - yh) * 8 + (mine + d) % 8)
    greet(inst, 15 - slab)
    for copy in small:
        copy.start()

    def state_copy(h, d):
        start, size = PIECES[h]
        p = peer(d)
        return pltpu.make_async_remote_copy(
            src_ref=x.at[:, pl.ds(pl.multiple_of(p * GRP + start, 16), size)],
            dst_ref=st_in.at[inst, :, pl.ds(start, size), :],
            send_sem=st_ssem.at[h, d],
            recv_sem=st_rsem.at[h, d],
            device_id={"inst": p, "slab": slab},
            device_id_type=MESH,
        )

    def amp_copy(d):
        return pltpu.make_async_remote_copy(
            src_ref=amp_out,
            dst_ref=amp_in.at[inst],
            send_sem=am_ssem.at[d],
            recv_sem=am_rsem.at[d],
            device_id={"inst": peer(d), "slab": slab},
            device_id_type=MESH,
        )

    def halo_copy(k):
        dst, to = ((0, slab + 1), (128, slab - 1))[k]
        return pltpu.make_async_remote_copy(
            src_ref=halo_out.at[k],
            dst_ref=halo.at[:, pl.ds(dst, 128)],
            send_sem=halo_ssem.at[k],
            recv_sem=halo_rsem.at[k],
            device_id={"inst": inst, "slab": to},
            device_id_type=MESH,
        )

    state_cp.wait()
    for dst, grp, k in ((ms_own, inst, 1), (ms_oth, inst_oth, 3)):
        ms_head(dst, grp, k).start()

        @pl.when(grp < 7)
        def _():
            ms_tail(dst, grp, k + 1).start()

        @pl.when(grp == 7)
        def _():
            dst[LAST:GRP] = jnp.zeros((GRP - LAST, 8, NE), BF16)
    xraw[NB:NBP] = jnp.zeros((NBP - NB, 8, 128), BF16)

    def split(g):
        rows = xraw[pl.ds(g * GRP, GRP)].astype(F32).reshape(GRP * 8, 128)
        xflat[...] = rows
        parts = {}
        for i in range(2):
            for c in range(4):
                part = xflat[pl.ds(c * 2 + i, GRP, stride=8), :]
                x[i, pl.ds(pl.multiple_of(g * GRP, 16), GRP), c * 128 : (c + 1) * 128] = part.astype(BF16)
                parts[c, i] = part
        rows = pl.ds(pl.multiple_of(g * GRP, 16), GRP)
        first = lax.broadcasted_iota(jnp.int32, (GRP, 128), 1) < 64
        high = jnp.where(first, pltpu.roll(parts[3, 0], 64, 1), parts[3, 1])
        low = jnp.where(first, parts[0, 0], pltpu.roll(parts[0, 1], 64, 1))
        halo_out[0, rows, :] = high.astype(BF16)
        halo_out[1, rows, :] = low.astype(BF16)

    pl.semaphore_wait(barrier, 23)
    for d in order:
        split(peer(d))
        for h in range(FIRST_PIECES):
            state_copy(h, d).start()
    split(inst)
    stiff_cp = local(stiff_hbm, stv, 5)
    stiff_cp.start()
    deriv_cp = local(deriv_hbm, dv, 6)
    deriv_cp.start()
    face_cp = local(face_hbm, fcv, 7)
    face_cp.start()
    precond_cp = local(precond_hbm, pcv, 9)
    precond_cp.start()
    @pl.when(slab == 0)
    def _():
        halo[:, 0:128] = jnp.zeros((NBP, 128), BF16)

    @pl.when(slab == 15)
    def _():
        halo[:, 128:256] = jnp.zeros((NBP, 128), BF16)

    for i in range(2):
        st_in[inst, i] = x[i, pl.ds(pl.multiple_of(inst * GRP, 16), GRP)]


    for copy in small:
        copy.wait()

    lane8 = lax.broadcasted_iota(jnp.int32, (8, 128), 1)
    row8 = lax.broadcasted_iota(jnp.int32, (8, 128), 0)
    tiled = jnp.zeros((8, 128), F32)
    amp = amp_ref[...]
    for j in range(2):
        for k in range(8):
            tiled = jnp.where((row8 == j) & (lane8 % 8 == k), amp[j : j + 1, k : k + 1], tiled)
    amp_out[...] = tiled
    amp_in[inst] = tiled

    for d in order:
        amp_copy(d).start()

    own = jnp.concatenate([owner_ref[pl.ds(c, 16, stride=4), :] for c in range(4)], axis=1)
    target = own // NE
    element = own - target * NE
    row16 = lax.broadcasted_iota(jnp.int32, (16, NE), 0)
    my_target = jnp.sum(jnp.where(row16 == slab, target, 0), axis=0, keepdims=True)
    up_r = lax.broadcasted_iota(jnp.int32, (NE, NE), 0)
    up_c = lax.broadcasted_iota(jnp.int32, (NE, NE), 1)
    upper = jnp.where(up_r < up_c, 1.0, 0.0).astype(BF16)
    match = jnp.where(row16 == my_target, 1.0, 0.0)
    before = dot(match.astype(BF16), upper)
    rank = jnp.sum(match * before, axis=0, keepdims=True)
    slot = my_target * 32 + rank.astype(jnp.int32)
    s_iota = lax.broadcasted_iota(jnp.int32, (256, NE), 0)
    pick_own = jnp.where(s_iota + yh * 256 == slot, 1.0, 0.0).astype(BF16)
    pick_oth = jnp.where(s_iota + (1 - yh) * 256 == slot, 1.0, 0.0).astype(BF16)

    for dst, grp, k in ((ms_own, inst, 1), (ms_oth, inst_oth, 3)):
        ms_head(dst, grp, k).wait()

        @pl.when(grp < 7)
        def _():
            ms_tail(dst, grp, k + 1).wait()

    snd_own[...] = dot_nt(pick_own, ms_own[...].astype(F32).reshape(GRP * 8, NE).astype(BF16)).astype(BF16)
    snd_oth[...] = dot_nt(pick_oth, ms_oth[...].astype(F32).reshape(GRP * 8, NE).astype(BF16)).astype(BF16)

    def ms_copy(d, other):
        idx = (mine + d) % 8
        src = snd_oth if other else snd_own
        return pltpu.make_async_remote_copy(
            src_ref=src.at[pl.ds(pl.multiple_of(idx * 32, 32), 32), :],
            dst_ref=ms_in.at[pl.ds(pl.multiple_of(slab * 32, 32), 32), :],
            send_sem=ms_ssem.at[int(other), d],
            recv_sem=ms_rsem.at[int(other), d],
            device_id={
                "inst": inst_oth if other else inst,
                "slab": ((1 - yh) if other else yh) * 8 + idx,
            },
            device_id_type=MESH,
        )


    for d in range(8):
        ms_copy(d, True).start()
    for d in range(1, 8):
        ms_copy(d, False).start()
    for h in range(FIRST_PIECES, len(PIECES)):
        for d in order:
            state_copy(h, d).start()

    @pl.when(slab < 15)
    def _():
        halo_copy(0).start()

    @pl.when(slab > 0)
    def _():
        halo_copy(1).start()
    ms_self = local(
        snd_own.at[pl.ds(pl.multiple_of(mine * 32, 32), 32), :],
        ms_in.at[pl.ds(pl.multiple_of(slab * 32, 32), 32), :],
        8,
    )
    ms_self.start()

    hits = jnp.where(target == slab, 1.0, 0.0)
    ranks = dot(hits.astype(BF16), upper)
    ranks = jnp.where(hits > 0.5, ranks, -1.0)
    element_f = element.astype(F32)
    c_iota = lax.broadcasted_iota(jnp.int32, (32, NE), 0).astype(F32)
    e_iota = lax.broadcasted_iota(jnp.int32, (32, NE), 1).astype(F32)
    for s in range(16):
        found = jnp.where(ranks[s : s + 1, :] == c_iota, element_f[s : s + 1, :], 0.0)
        column = jnp.sum(found, axis=1, keepdims=True)
        placing[32 * s : 32 * s + 32, :] = jnp.where(column == e_iota, 1.0, 0.0).astype(BF16)

    links = links_ref[...]
    inner = jnp.where((links >= 64) & (links < 576), links - 64, -1)
    outer = jnp.where(links < 64, links, jnp.where(links < 576, -256, links - 448))

    def half_face(u):
        f, i = u // 2, u % 2
        span = lax.broadcasted_iota(jnp.int32, (NE, NE), 0)
        if i == 0:
            sel[...] = jnp.where(span == inner[f : f + 1, :], 1.0, 0.0).astype(BF16)
        edge = jnp.where(span[0:256] == outer[f : f + 1, :] + 64 * i, 1.0, 0.0).astype(BF16)
        picked = (dot(x[i], sel[...]) + dot(halo[...], edge)).astype(BF16)
        acc[i, 0:NB] += dot(fcv[f], picked[0:NB])

    acc[:, NB:NBP] = jnp.zeros((2, NBP - NB, NE), F32)
    stiff_cp.wait()
    for i in range(2):
        acc[i, 0:NB] = dot(stv[...], x[i, 0:NB])

    for d in order:
        amp_copy(d).wait_recv()
    a_all = jnp.concatenate([amp_in[p, 0:2] for p in range(8)], axis=0)
    a_all = jnp.broadcast_to(a_all[:, None, :], (16, 16, 128)).reshape(256, 128)
    k_row = lax.broadcasted_iota(jnp.int32, (256, 128), 0) % 16
    k_col = lax.broadcasted_iota(jnp.int32, (256, 128), 1) // 8
    a_all = jnp.where(k_row == k_col, a_all, 0.0)
    a_high = a_all.astype(BF16)
    a_low = (a_all - a_high.astype(F32)).astype(BF16)
    a_both = jnp.concatenate([a_high, a_low], axis=1)

    ms_self.wait()
    for d in range(8):
        ms_copy(d, True).wait_recv()
    for d in range(1, 8):
        ms_copy(d, False).wait_recv()
    for q in range(5):
        rows = ms_in[:, 128 * q : 128 * q + 128]
        deflection = dot_nt(a_both, jnp.concatenate([rows, rows], axis=1)).astype(BF16)
        forcing[q] = dot(deflection, placing[...])

    face_cp.wait()

    @pl.when(slab > 0)
    def _():
        halo_copy(0).wait_recv()

    @pl.when(slab < 15)
    def _():
        halo_copy(1).wait_recv()

    for u in range(PLAN[0]):
        half_face(u)

    deriv_cp.wait()
    volume = jnp.concatenate([volume_ref[c : c + 1, :] for c in range(4)], axis=1)

    def ret_copy(h, d):
        start, size = PIECES[h]
        p = peer(d)
        return pltpu.make_async_remote_copy(
            src_ref=ret_out.at[p, :, pl.ds(start, size), :],
            dst_ref=ret_in.at[inst, :, pl.ds(start, size), :],
            send_sem=rt_ssem.at[h, d],
            recv_sem=rt_rsem.at[h, d],
            device_id={"inst": p, "slab": slab},
            device_id_type=MESH,
        )

    for h in range(len(PIECES)):
        for d in order:
            state_copy(h, d).wait_recv()
        start, size = PIECES[h]
        for q in range(start // 16, (start + size) // 16):
            block = st_in[:, :, 16 * q : 16 * q + 16, :].reshape(256, NE)
            spectral = dot(dv[0], block) + dot(dv[1], block)
            back = (volume * spectral - forcing[q]).astype(BF16)
            ret_out[:, :, 16 * q : 16 * q + 16, :] = back.reshape(8, 2, 16, NE)
        for d in order:
            ret_copy(h, d).start()
        if h == 0:
            for u in range(PLAN[0], PLAN[0] + PLAN[1]):
                half_face(u)

    for i in range(2):
        ret_in[inst, i] = ret_out[inst, i]

    for u in range(PLAN[0] + PLAN[1], 12):
        half_face(u)

    precond_cp.wait()
    p_row = lax.broadcasted_iota(jnp.int32, (NB, NBP), 0)
    p_col = lax.broadcasted_iota(jnp.int32, (NB, NBP), 1)
    p_first = GRP * (p_col // 48) + p_col % 48
    p_second = GRP * ((p_col - 384) // 32) + 48 + (p_col - 384) % 32
    moved = jnp.where(p_row == jnp.where(p_col < 384, p_first, p_second), 1.0, 0.0).astype(BF16)
    pc_cols[...] = dot(pcv[...], moved).astype(BF16)

    for h in range(2):
        start, size = TAIL[h]
        for k, (piece, _) in enumerate(PIECES):
            if start <= piece < start + size:
                for d in order:
                    ret_copy(k, d).wait_recv()
        base = 384 * h
        for i in range(2):
            for g in range(8):
                row = g * GRP + start
                total = acc[i, row : row + size] + ret_in[g, i, start : start + size].astype(F32)
                rounded[i, base + g * size : base + (g + 1) * size] = total.astype(BF16)
                count = min(size, NB - row)
                for c in range(4):
                    res_ref[pl.ds(row * 8 + c * 2 + i, count, stride=8), :] = total[
                        0:count, c * 128 : (c + 1) * 128
                    ]
            if h == 0:
                change[i] = dot(pc_cols[:, 0:384], rounded[i, 0:384])

    for d in order:
        amp_copy(d).wait_send()
        for h in range(len(PIECES)):
            state_copy(h, d).wait_send()
            ret_copy(h, d).wait_send()
    for d in range(8):
        ms_copy(d, True).wait_send()
    for d in range(1, 8):
        ms_copy(d, False).wait_send()

    @pl.when(slab < 15)
    def _():
        halo_copy(0).wait_send()

    @pl.when(slab > 0)
    def _():
        halo_copy(1).wait_send()


CHUNKS = ((0, 320), (320, 305))


def finish_kernel(res_in, change, rounded, pc_cols, x, step_ref, res_hbm, new_hbm, new, sem):
    copies = [
        pltpu.make_async_copy(res_in.at[pl.ds(8 * b, 8 * n)], res_hbm.at[pl.ds(8 * b, 8 * n)], sem.at[0, k])
        for k, (b, n) in enumerate(CHUNKS)
    ]
    for copy in copies:
        copy.start()
    for k, (b, n) in enumerate(CHUNKS):
        for i in range(2):
            part = dot(pc_cols[b : b + n, 384:640], rounded[i, 384:640]) + change[i, b : b + n]
            for c in range(4):
                lanes = slice(c * 128, (c + 1) * 128)
                value = x[i, b : b + n, lanes].astype(F32) - step_ref[c : c + 1, :] * part[:, lanes]
                new[pl.ds(8 * b + c * 2 + i, n, stride=8), :] = value
        copy = pltpu.make_async_copy(new.at[pl.ds(8 * b, 8 * n)], new_hbm.at[pl.ds(8 * b, 8 * n)], sem.at[1, k])
        copy.start()
        copies.append(copy)
    for copy in copies:
        copy.wait()


def body(state, volume, step_size, stiffness, face_coupling, precond, mode_shapes, amplitudes, surface_owner, face_links):
    raw = state.reshape(2, NB, 4, 128).transpose(1, 2, 0, 3).reshape(NB, 8, 128)
    shapes = mode_shapes.transpose(1, 0, 2)
    any_spec = pl.BlockSpec(memory_space=pl.ANY)
    vmem = pl.BlockSpec(memory_space=pltpu.VMEM)
    dma = pltpu.SemaphoreType.DMA
    held = pl.pallas_call(
        gather_kernel,
        out_shape=[
            pltpu.VMEM((NB * 8, 128), F32),
            pltpu.VMEM((2, NB, NE), F32),
            pltpu.VMEM((2, NBP, NE), BF16),
            pltpu.VMEM((NB, NBP), BF16),
            pltpu.VMEM((2, NBP, NE), BF16),
        ],
        in_specs=[any_spec] * 10,
        out_specs=[vmem] * 5,
        scratch_shapes=[
            pltpu.VMEM((4, 128), F32),
            pltpu.VMEM((2, 8), F32),
            pltpu.VMEM((64, 128), jnp.int32),
            pltpu.VMEM((6, NE), jnp.int32),
            pltpu.VMEM((2, NBP, NE), F32),
            pltpu.VMEM((NB, NB), BF16),
            pltpu.VMEM((NBP, 8, 128), BF16),
            pltpu.VMEM((GRP * 8, 128), F32),
            pltpu.VMEM((NBP, 256), BF16),
            pltpu.VMEM((2, NBP, 128), BF16),
            pltpu.VMEM((8, 2, GRP, NE), BF16),
            pltpu.VMEM((GRP, 8, NE), BF16),
            pltpu.VMEM((GRP, 8, NE), BF16),
            pltpu.VMEM((256, GRP * 8), BF16),
            pltpu.VMEM((256, GRP * 8), BF16),
            pltpu.VMEM((512, GRP * 8), BF16),
            pltpu.VMEM((8, 2, GRP, NE), BF16),
            pltpu.VMEM((8, 2, GRP, NE), BF16),
            pltpu.VMEM((8, 128), F32),
            pltpu.VMEM((8, 8, 128), F32),
            pltpu.VMEM((6, NB, NB), BF16),
            pltpu.VMEM((NB, NB), BF16),
            pltpu.VMEM((2, 256, 256), BF16),
            pltpu.VMEM((NE, NE), BF16),
            pltpu.VMEM((512, NE), BF16),
            pltpu.VMEM((5, 256, NE), F32),
            dma((15,)),
            dma((len(PIECES), 8)),
            dma((len(PIECES), 8)),
            dma((len(PIECES), 8)),
            dma((len(PIECES), 8)),
            dma((2, 8)),
            dma((2, 8)),
            dma((8,)),
            dma((8,)),
            dma((2,)),
            dma((2,)),
        ],
        compiler_params=pltpu.CompilerParams(
            collective_id=0, has_side_effects=True, vmem_limit_bytes=54 << 20
        ),
        cost_estimate=pl.CostEstimate(flops=13_000_000_000, bytes_accessed=16_000_000, transcendentals=0),
    )(
        raw,
        shapes,
        stiffness,
        face_coupling,
        precond,
        jnp.asarray(derivative_blocks()),
        volume.reshape(4, 128),
        amplitudes,
        surface_owner.reshape(64, 128),
        face_links,
    )
    res_raw, new_raw = pl.pallas_call(
        finish_kernel,
        out_shape=[jax.ShapeDtypeStruct((NB * 8, 128), F32)] * 2,
        in_specs=[vmem] * 6,
        out_specs=[any_spec] * 2,
        scratch_shapes=[pltpu.VMEM((NB * 8, 128), F32), dma((2, 2))],
        compiler_params=pltpu.CompilerParams(vmem_limit_bytes=10 << 20),
        cost_estimate=pl.CostEstimate(flops=330_000_000, bytes_accessed=5_000_000, transcendentals=0),
    )(*[pltpu.with_memory_space_constraint(a, pltpu.VMEM) for a in held], step_size.reshape(4, 128))

    def whole(a):
        return a.reshape(NB, 4, 2, 128).transpose(2, 0, 1, 3).reshape(2, NB, NE)

    return whole(res_raw), whole(new_raw)


def solution(mesh):
    return jax.shard_map(
        body,
        mesh=mesh,
        in_specs=(
            P("inst", None, "slab"),
            P("slab"),
            P("slab"),
            P(),
            P(),
            P(),
            P(None, None, "slab"),
            P("inst", None),
            P(),
            P(None, "slab"),
        ),
        out_specs=(P("inst", None, "slab"), P("inst", None, "slab")),
        check_vma=False,
    )
```

```python
import functools

import jax
import jax.numpy as jnp
import numpy as np
from jax import lax
from jax.experimental import pallas as pl
from jax.experimental.pallas import tpu as pltpu
from jax.sharding import PartitionSpec as P

MESH = pl.DeviceIdType.MESH
F32, BF16 = jnp.float32, jnp.bfloat16

NB = 625
NBP = 640
GRP = 80
LAST = NB - 7 * GRP
NE = 512
PIECES = ((0, 48), (48, 32))
TAIL = ((0, 48), (48, 32))
FIRST_PIECES = 1
PLAN = (0, 4, 8)


def derivative_blocks():
    n = np.arange(16)
    d = n[:, None] - n[None, :]
    safe = np.where(d == 0, 1, d)
    value = np.where(d == 0, 0.0, 0.2 * (-1.0) ** d / np.tan(np.pi * safe / 16))
    value = np.kron(value, np.eye(16)).astype(np.float32)
    high = value.astype(jnp.bfloat16)
    low = (value - high.astype(np.float32)).astype(jnp.bfloat16)
    return np.stack([high, low])


def dot(a, b):
    return jnp.dot(a, b, preferred_element_type=F32)


def dot_nt(a, b):
    return lax.dot_general(a, b, (((1,), (1,)), ((), ())), preferred_element_type=F32)


def gather_kernel(
    state_hbm,
    ms_hbm,
    stiff_hbm,
    face_hbm,
    precond_hbm,
    deriv_hbm,
    volume_hbm,
    amp_hbm,
    owner_hbm,
    links_hbm,
    res_ref,
    change,
    rounded,
    pc_cols,
    x,
    volume_ref,
    amp_ref,
    owner_ref,
    links_ref,
    acc,
    pcv,
    xraw,
    xflat,
    halo,
    halo_out,
    st_in,
    ms_own,
    ms_oth,
    snd_own,
    snd_oth,
    ms_in,
    ret_out,
    ret_in,
    amp_out,
    amp_in,
    fcv,
    stv,
    dv,
    sel,
    placing,
    forcing,
    local_sem,
    st_ssem,
    st_rsem,
    rt_ssem,
    rt_rsem,
    ms_ssem,
    ms_rsem,
    am_ssem,
    am_rsem,
    halo_ssem,
    halo_rsem,
):
    inst = lax.axis_index("inst")
    slab = lax.axis_index("slab")
    zz, yl = inst // 2, inst % 2
    yh, mine = slab // 8, slab % 8
    inst_oth = zz * 2 + (1 - yl)

    def local(src, dst, k):
        return pltpu.make_async_copy(src, dst, local_sem.at[k])

    state_cp = local(state_hbm, xraw.at[pl.ds(0, NB)], 0)
    state_cp.start()

    def ms_head(dst, grp, k):
        return local(ms_hbm.at[pl.ds(grp * GRP, LAST)], dst.at[pl.ds(0, LAST)], k)

    def ms_tail(dst, grp, k):
        return local(
            ms_hbm.at[pl.ds(grp * GRP + LAST, GRP - LAST)], dst.at[pl.ds(LAST, GRP - LAST)], k
        )

    small = [
        local(src, dst, 10 + k)
        for k, (src, dst) in enumerate(
            (
                (amp_hbm, amp_ref),
                (owner_hbm, owner_ref),
                (links_hbm, links_ref),
                (volume_hbm, volume_ref),
            )
        )
    ]

    def peer(d):
        return ((zz + d // 2) % 4) * 2 + (yl + d % 2) % 2

    order = (5, 3, 7, 4, 2, 6, 1)
    barrier = pltpu.get_barrier_semaphore()

    def greet(i, s):
        pl.semaphore_signal(barrier, inc=1, device_id={"inst": i, "slab": s}, device_id_type=MESH)

    for d in order:
        greet(peer(d), slab)
    for d in range(1, 8):
        greet(inst, yh * 8 + (mine + d) % 8)
    for d in range(8):
        greet(inst_oth, (1 - yh) * 8 + (mine + d) % 8)
    greet(inst, 15 - slab)
    for copy in small:
        copy.start()

    def state_copy(h, d):
        start, size = PIECES[h]
        p = peer(d)
        return pltpu.make_async_remote_copy(
            src_ref=x.at[:, pl.ds(pl.multiple_of(p * GRP + start, 16), size)],
            dst_ref=st_in.at[inst, :, pl.ds(start, size), :],
            send_sem=st_ssem.at[h, d],
            recv_sem=st_rsem.at[h, d],
            device_id={"inst": p, "slab": slab},
            device_id_type=MESH,
        )

    def amp_copy(d):
        return pltpu.make_async_remote_copy(
            src_ref=amp_out,
            dst_ref=amp_in.at[inst],
            send_sem=am_ssem.at[d],
            recv_sem=am_rsem.at[d],
            device_id={"inst": peer(d), "slab": slab},
            device_id_type=MESH,
        )

    def halo_copy(k):
        dst, to = ((0, slab + 1), (128, slab - 1))[k]
        return pltpu.make_async_remote_copy(
            src_ref=halo_out.at[k],
            dst_ref=halo.at[:, pl.ds(dst, 128)],
            send_sem=halo_ssem.at[k],
            recv_sem=halo_rsem.at[k],
            device_id={"inst": inst, "slab": to},
            device_id_type=MESH,
        )

    state_cp.wait()
    for dst, grp, k in ((ms_own, inst, 1), (ms_oth, inst_oth, 3)):
        ms_head(dst, grp, k).start()

        @pl.when(grp < 7)
        def _():
            ms_tail(dst, grp, k + 1).start()

        @pl.when(grp == 7)
        def _():
            dst[LAST:GRP] = jnp.zeros((GRP - LAST, 8, NE), BF16)
    xraw[NB:NBP] = jnp.zeros((NBP - NB, 8, 128), BF16)

    def split(g):
        rows = xraw[pl.ds(g * GRP, GRP)].astype(F32).reshape(GRP * 8, 128)
        xflat[...] = rows
        parts = {}
        for i in range(2):
            for c in range(4):
                part = xflat[pl.ds(c * 2 + i, GRP, stride=8), :]
                x[i, pl.ds(pl.multiple_of(g * GRP, 16), GRP), c * 128 : (c + 1) * 128] = part.astype(BF16)
                parts[c, i] = part
        rows = pl.ds(pl.multiple_of(g * GRP, 16), GRP)
        first = lax.broadcasted_iota(jnp.int32, (GRP, 128), 1) < 64
        high = jnp.where(first, pltpu.roll(parts[3, 0], 64, 1), parts[3, 1])
        low = jnp.where(first, parts[0, 0], pltpu.roll(parts[0, 1], 64, 1))
        halo_out[0, rows, :] = high.astype(BF16)
        halo_out[1, rows, :] = low.astype(BF16)

    pl.semaphore_wait(barrier, 23)
    for d in order:
        split(peer(d))
        for h in range(FIRST_PIECES):
            state_copy(h, d).start()
    split(inst)
    stiff_cp = local(stiff_hbm, stv, 5)
    stiff_cp.start()
    deriv_cp = local(deriv_hbm, dv, 6)
    deriv_cp.start()
    face_cp = local(face_hbm, fcv, 7)
    face_cp.start()
    precond_cp = local(precond_hbm, pcv, 9)
    precond_cp.start()
    @pl.when(slab == 0)
    def _():
        halo[:, 0:128] = jnp.zeros((NBP, 128), BF16)

    @pl.when(slab == 15)
    def _():
        halo[:, 128:256] = jnp.zeros((NBP, 128), BF16)

    for i in range(2):
        st_in[inst, i] = x[i, pl.ds(pl.multiple_of(inst * GRP, 16), GRP)]


    for copy in small:
        copy.wait()

    lane8 = lax.broadcasted_iota(jnp.int32, (8, 128), 1)
    row8 = lax.broadcasted_iota(jnp.int32, (8, 128), 0)
    tiled = jnp.zeros((8, 128), F32)
    amp = amp_ref[...]
    for j in range(2):
        for k in range(8):
            tiled = jnp.where((row8 == j) & (lane8 % 8 == k), amp[j : j + 1, k : k + 1], tiled)
    amp_out[...] = tiled
    amp_in[inst] = tiled

    for d in order:
        amp_copy(d).start()

    own = jnp.concatenate([owner_ref[pl.ds(c, 16, stride=4), :] for c in range(4)], axis=1)
    target = own // NE
    element = own - target * NE
    row16 = lax.broadcasted_iota(jnp.int32, (16, NE), 0)
    my_target = jnp.sum(jnp.where(row16 == slab, target, 0), axis=0, keepdims=True)
    up_r = lax.broadcasted_iota(jnp.int32, (NE, NE), 0)
    up_c = lax.broadcasted_iota(jnp.int32, (NE, NE), 1)
    upper = jnp.where(up_r < up_c, 1.0, 0.0).astype(BF16)
    match = jnp.where(row16 == my_target, 1.0, 0.0)
    before = dot(match.astype(BF16), upper)
    rank = jnp.sum(match * before, axis=0, keepdims=True)
    slot = my_target * 32 + rank.astype(jnp.int32)
    s_iota = lax.broadcasted_iota(jnp.int32, (256, NE), 0)
    pick_own = jnp.where(s_iota + yh * 256 == slot, 1.0, 0.0).astype(BF16)
    pick_oth = jnp.where(s_iota + (1 - yh) * 256 == slot, 1.0, 0.0).astype(BF16)

    for dst, grp, k in ((ms_own, inst, 1), (ms_oth, inst_oth, 3)):
        ms_head(dst, grp, k).wait()

        @pl.when(grp < 7)
        def _():
            ms_tail(dst, grp, k + 1).wait()

    snd_own[...] = dot_nt(pick_own, ms_own[...].astype(F32).reshape(GRP * 8, NE).astype(BF16)).astype(BF16)
    snd_oth[...] = dot_nt(pick_oth, ms_oth[...].astype(F32).reshape(GRP * 8, NE).astype(BF16)).astype(BF16)

    def ms_copy(d, other):
        idx = (mine + d) % 8
        src = snd_oth if other else snd_own
        return pltpu.make_async_remote_copy(
            src_ref=src.at[pl.ds(pl.multiple_of(idx * 32, 32), 32), :],
            dst_ref=ms_in.at[pl.ds(pl.multiple_of(slab * 32, 32), 32), :],
            send_sem=ms_ssem.at[int(other), d],
            recv_sem=ms_rsem.at[int(other), d],
            device_id={
                "inst": inst_oth if other else inst,
                "slab": ((1 - yh) if other else yh) * 8 + idx,
            },
            device_id_type=MESH,
        )


    for d in range(8):
        ms_copy(d, True).start()
    for d in range(1, 8):
        ms_copy(d, False).start()
    for h in range(FIRST_PIECES, len(PIECES)):
        for d in order:
            state_copy(h, d).start()

    @pl.when(slab < 15)
    def _():
        halo_copy(0).start()

    @pl.when(slab > 0)
    def _():
        halo_copy(1).start()
    ms_self = local(
        snd_own.at[pl.ds(pl.multiple_of(mine * 32, 32), 32), :],
        ms_in.at[pl.ds(pl.multiple_of(slab * 32, 32), 32), :],
        8,
    )
    ms_self.start()

    hits = jnp.where(target == slab, 1.0, 0.0)
    ranks = dot(hits.astype(BF16), upper)
    ranks = jnp.where(hits > 0.5, ranks, -1.0)
    element_f = element.astype(F32)
    c_iota = lax.broadcasted_iota(jnp.int32, (32, NE), 0).astype(F32)
    e_iota = lax.broadcasted_iota(jnp.int32, (32, NE), 1).astype(F32)
    for s in range(16):
        found = jnp.where(ranks[s : s + 1, :] == c_iota, element_f[s : s + 1, :], 0.0)
        column = jnp.sum(found, axis=1, keepdims=True)
        placing[32 * s : 32 * s + 32, :] = jnp.where(column == e_iota, 1.0, 0.0).astype(BF16)

    links = links_ref[...]
    inner = jnp.where((links >= 64) & (links < 576), links - 64, -1)
    outer = jnp.where(links < 64, links, jnp.where(links < 576, -256, links - 448))

    def half_face(u):
        f, i = u // 2, u % 2
        span = lax.broadcasted_iota(jnp.int32, (NE, NE), 0)
        if i == 0:
            sel[...] = jnp.where(span == inner[f : f + 1, :], 1.0, 0.0).astype(BF16)
        edge = jnp.where(span[0:256] == outer[f : f + 1, :] + 64 * i, 1.0, 0.0).astype(BF16)
        picked = (dot(x[i], sel[...]) + dot(halo[...], edge)).astype(BF16)
        acc[i, 0:NB] += dot(fcv[f], picked[0:NB])

    acc[:, NB:NBP] = jnp.zeros((2, NBP - NB, NE), F32)
    stiff_cp.wait()
    for i in range(2):
        acc[i, 0:NB] = dot(stv[...], x[i, 0:NB])

    for d in order:
        amp_copy(d).wait_recv()
    a_all = jnp.concatenate([amp_in[p, 0:2] for p in range(8)], axis=0)
    a_all = jnp.broadcast_to(a_all[:, None, :], (16, 16, 128)).reshape(256, 128)
    k_row = lax.broadcasted_iota(jnp.int32, (256, 128), 0) % 16
    k_col = lax.broadcasted_iota(jnp.int32, (256, 128), 1) // 8
    a_all = jnp.where(k_row == k_col, a_all, 0.0)
    a_high = a_all.astype(BF16)
    a_low = (a_all - a_high.astype(F32)).astype(BF16)
    a_both = jnp.concatenate([a_high, a_low], axis=1)

    ms_self.wait()
    for d in range(8):
        ms_copy(d, True).wait_recv()
    for d in range(1, 8):
        ms_copy(d, False).wait_recv()
    for q in range(5):
        rows = ms_in[:, 128 * q : 128 * q + 128]
        deflection = dot_nt(a_both, jnp.concatenate([rows, rows], axis=1)).astype(BF16)
        forcing[q] = dot(deflection, placing[...])

    face_cp.wait()

    @pl.when(slab > 0)
    def _():
        halo_copy(0).wait_recv()

    @pl.when(slab < 15)
    def _():
        halo_copy(1).wait_recv()

    for u in range(PLAN[0]):
        half_face(u)

    deriv_cp.wait()
    volume = jnp.concatenate([volume_ref[c : c + 1, :] for c in range(4)], axis=1)

    def ret_copy(h, d):
        start, size = PIECES[h]
        p = peer(d)
        return pltpu.make_async_remote_copy(
            src_ref=ret_out.at[p, :, pl.ds(start, size), :],
            dst_ref=ret_in.at[inst, :, pl.ds(start, size), :],
            send_sem=rt_ssem.at[h, d],
            recv_sem=rt_rsem.at[h, d],
            device_id={"inst": p, "slab": slab},
            device_id_type=MESH,
        )

    for h in range(len(PIECES)):
        for d in order:
            state_copy(h, d).wait_recv()
        start, size = PIECES[h]
        for q in range(start // 16, (start + size) // 16):
            block = st_in[:, :, 16 * q : 16 * q + 16, :].reshape(256, NE)
            spectral = dot(dv[0], block) + dot(dv[1], block)
            back = (volume * spectral - forcing[q]).astype(BF16)
            ret_out[:, :, 16 * q : 16 * q + 16, :] = back.reshape(8, 2, 16, NE)
        for d in order:
            ret_copy(h, d).start()
        if h == 0:
            for u in range(PLAN[0], PLAN[0] + PLAN[1]):
                half_face(u)

    for i in range(2):
        ret_in[inst, i] = ret_out[inst, i]

    for u in range(PLAN[0] + PLAN[1], 12):
        half_face(u)

    precond_cp.wait()
    p_row = lax.broadcasted_iota(jnp.int32, (NB, NBP), 0)
    p_col = lax.broadcasted_iota(jnp.int32, (NB, NBP), 1)
    p_first = GRP * (p_col // 48) + p_col % 48
    p_second = GRP * ((p_col - 384) // 32) + 48 + (p_col - 384) % 32
    moved = jnp.where(p_row == jnp.where(p_col < 384, p_first, p_second), 1.0, 0.0).astype(BF16)
    pc_cols[...] = dot(pcv[...], moved).astype(BF16)

    for h in range(2):
        start, size = TAIL[h]
        for k, (piece, _) in enumerate(PIECES):
            if start <= piece < start + size:
                for d in order:
                    ret_copy(k, d).wait_recv()
        base = 384 * h
        for i in range(2):
            for g in range(8):
                row = g * GRP + start
                total = acc[i, row : row + size] + ret_in[g, i, start : start + size].astype(F32)
                rounded[i, base + g * size : base + (g + 1) * size] = total.astype(BF16)
                count = min(size, NB - row)
                for c in range(4):
                    res_ref[pl.ds(row * 8 + c * 2 + i, count, stride=8), :] = total[
                        0:count, c * 128 : (c + 1) * 128
                    ]
            if h == 0:
                change[i] = dot(pc_cols[:, 0:384], rounded[i, 0:384])

    for d in order:
        amp_copy(d).wait_send()
        for h in range(len(PIECES)):
            state_copy(h, d).wait_send()
            ret_copy(h, d).wait_send()
    for d in range(8):
        ms_copy(d, True).wait_send()
    for d in range(1, 8):
        ms_copy(d, False).wait_send()

    @pl.when(slab < 15)
    def _():
        halo_copy(0).wait_send()

    @pl.when(slab > 0)
    def _():
        halo_copy(1).wait_send()


CHUNKS = ((0, 320), (320, 305))


def finish_kernel(res_in, change, rounded, pc_cols, x, step_ref, res_hbm, new_hbm, new, sem):
    copies = [
        pltpu.make_async_copy(res_in.at[pl.ds(8 * b, 8 * n)], res_hbm.at[pl.ds(8 * b, 8 * n)], sem.at[0, k])
        for k, (b, n) in enumerate(CHUNKS)
    ]
    for copy in copies:
        copy.start()
    for k, (b, n) in enumerate(CHUNKS):
        for i in range(2):
            part = dot(pc_cols[b : b + n, 384:640], rounded[i, 384:640]) + change[i, b : b + n]
            for c in range(4):
                lanes = slice(c * 128, (c + 1) * 128)
                value = x[i, b : b + n, lanes].astype(F32) - step_ref[c : c + 1, :] * part[:, lanes]
                new[pl.ds(8 * b + c * 2 + i, n, stride=8), :] = value
        copy = pltpu.make_async_copy(new.at[pl.ds(8 * b, 8 * n)], new_hbm.at[pl.ds(8 * b, 8 * n)], sem.at[1, k])
        copy.start()
        copies.append(copy)
    for copy in copies:
        copy.wait()


def body(state, volume, step_size, stiffness, face_coupling, precond, mode_shapes, amplitudes, surface_owner, face_links):
    raw = state.reshape(2, NB, 4, 128).transpose(1, 2, 0, 3).reshape(NB, 8, 128)
    shapes = mode_shapes.transpose(1, 0, 2)
    any_spec = pl.BlockSpec(memory_space=pl.ANY)
    vmem = pl.BlockSpec(memory_space=pltpu.VMEM)
    dma = pltpu.SemaphoreType.DMA
    held = pl.pallas_call(
        gather_kernel,
        out_shape=[
            pltpu.VMEM((NB * 8, 128), F32),
            pltpu.VMEM((2, NB, NE), F32),
            pltpu.VMEM((2, NBP, NE), BF16),
            pltpu.VMEM((NB, NBP), BF16),
            pltpu.VMEM((2, NBP, NE), BF16),
        ],
        in_specs=[any_spec] * 10,
        out_specs=[vmem] * 5,
        scratch_shapes=[
            pltpu.VMEM((4, 128), F32),
            pltpu.VMEM((2, 8), F32),
            pltpu.VMEM((64, 128), jnp.int32),
            pltpu.VMEM((6, NE), jnp.int32),
            pltpu.VMEM((2, NBP, NE), F32),
            pltpu.VMEM((NB, NB), BF16),
            pltpu.VMEM((NBP, 8, 128), BF16),
            pltpu.VMEM((GRP * 8, 128), F32),
            pltpu.VMEM((NBP, 256), BF16),
            pltpu.VMEM((2, NBP, 128), BF16),
            pltpu.VMEM((8, 2, GRP, NE), BF16),
            pltpu.VMEM((GRP, 8, NE), BF16),
            pltpu.VMEM((GRP, 8, NE), BF16),
            pltpu.VMEM((256, GRP * 8), BF16),
            pltpu.VMEM((256, GRP * 8), BF16),
            pltpu.VMEM((512, GRP * 8), BF16),
            pltpu.VMEM((8, 2, GRP, NE), BF16),
            pltpu.VMEM((8, 2, GRP, NE), BF16),
            pltpu.VMEM((8, 128), F32),
            pltpu.VMEM((8, 8, 128), F32),
            pltpu.VMEM((6, NB, NB), BF16),
            pltpu.VMEM((NB, NB), BF16),
            pltpu.VMEM((2, 256, 256), BF16),
            pltpu.VMEM((NE, NE), BF16),
            pltpu.VMEM((512, NE), BF16),
            pltpu.VMEM((5, 256, NE), F32),
            dma((15,)),
            dma((len(PIECES), 8)),
            dma((len(PIECES), 8)),
            dma((len(PIECES), 8)),
            dma((len(PIECES), 8)),
            dma((2, 8)),
            dma((2, 8)),
            dma((8,)),
            dma((8,)),
            dma((2,)),
            dma((2,)),
        ],
        compiler_params=pltpu.CompilerParams(
            collective_id=0, has_side_effects=True, vmem_limit_bytes=54 << 20
        ),
        cost_estimate=pl.CostEstimate(flops=13_000_000_000, bytes_accessed=16_000_000, transcendentals=0),
    )(
        raw,
        shapes,
        stiffness,
        face_coupling,
        precond,
        jnp.asarray(derivative_blocks()),
        volume.reshape(4, 128),
        amplitudes,
        surface_owner.reshape(64, 128),
        face_links,
    )
    res_raw, new_raw = pl.pallas_call(
        finish_kernel,
        out_shape=[jax.ShapeDtypeStruct((NB * 8, 128), F32)] * 2,
        in_specs=[vmem] * 6,
        out_specs=[any_spec] * 2,
        scratch_shapes=[pltpu.VMEM((NB * 8, 128), F32), dma((2, 2))],
        compiler_params=pltpu.CompilerParams(vmem_limit_bytes=10 << 20),
        cost_estimate=pl.CostEstimate(flops=330_000_000, bytes_accessed=5_000_000, transcendentals=0),
    )(*[pltpu.with_memory_space_constraint(a, pltpu.VMEM) for a in held], step_size.reshape(4, 128))

    def whole(a):
        return a.reshape(NB, 4, 2, 128).transpose(2, 0, 1, 3).reshape(2, NB, NE)

    return whole(res_raw), whole(new_raw)


def solution(mesh):
    return jax.shard_map(
        body,
        mesh=mesh,
        in_specs=(
            P("inst", None, "slab"),
            P("slab"),
            P("slab"),
            P(),
            P(),
            P(),
            P(None, None, "slab"),
            P("inst", None),
            P(),
            P(None, "slab"),
        ),
        out_specs=(P("inst", None, "slab"), P("inst", None, "slab")),
        check_vma=False,
    )
```
